128 devices in a mesh: gx: 8 (over z_lo, x), gy: 16 (over z_hi, y, core).
Axes of the slice: x: 4, y: 4, z: 4 (z_hi: 2, z_lo: 2; z = z_hi * 2 + z_lo), core: 2. Of those that a mesh axis runs over, the one named last changes fastest.
Arguments:
- initial_state: float32 [4, 4, 32, 128, 1024], P(None, None, None, 'gy', 'gx'), may hold values from -6 to 6
- forcing: float32 [4, 4, 32, 128, 1024], P(None, None, None, 'gy', 'gx'), may hold values from -6 to 6
- jacobian: float32 [4, 4, 128, 1024], P(None, None, 'gy', 'gx'), may hold values from 0.5 to 2
- metric: float32 [4, 4, 128, 1024], P(None, None, 'gy', 'gx'), may hold values from 0.5 to 2
- viscosity: float32 [32], replicated, may hold values from 0.0001 to 0.0006
- element_turns: int32 [128, 1024], P('gy', 'gx'), may hold values from 0 to 3
Outputs:
- final_state: float32 [4, 4, 32, 128, 1024], P(None, None, None, 'gy', 'gx')
The draws below stay inside these ranges and needn't reach their ends.
Inputs may be any that keep to these rules, and one draw needn't show every extreme that they name: `element_turns`: quarter turns from an element's stored node order to its face's node order.
All inputs are finite; a program needn't handle non-finite values.
Results may differ from the reference program's by a relative error of at most 0.0001.
Values sent between devices are 32-bit elements; how exact they have to be, the bound alone decides.
A program may use at most 128 MiB of HBM per device.

```python
import math
import jax
import jax.numpy as jnp
import numpy as np
from jax import lax

NP = 4
SECTIONS = 5
CHAN = 32
ELX = 1024
ELY = 128


def touch_ends(values, own_key, low, largest):
    longest = values.shape.index(max(values.shape))
    spots = []
    for shift in (0, 1):
        where = [jax.random.randint(jax.random.fold_in(own_key, axis), (), 0, length) for axis, length in enumerate(values.shape)]
        where[longest] = (where[longest] + shift) % values.shape[longest]
        spots.append(tuple(where))
    return values.at[spots[0]].set(low).at[spots[1]].set(largest)


def level_of(stream_key, shape, pieces, least, top_value):
    loudness = 1.0
    for axis_at, shards_of in pieces:
        steps = jax.random.uniform(jax.random.fold_in(jax.random.fold_in(stream_key, 6), axis_at), (shards_of,), jnp.float32, least / len(pieces), top_value / len(pieces))
        loudness = loudness * jnp.repeat(jnp.exp(steps), shape[axis_at] // shards_of).reshape((-1,) + (1,) * (len(shape) - 1 - axis_at))
    return loudness


def normal_values(rng, dims, deviation, reach, split=(), kind=jnp.bfloat16):
    entries = jax.random.normal(rng, dims, jnp.float32) * deviation
    if len(split) > 0:
        entries = level_of(rng, dims, split, -0.22, 0.18) * entries
    return jnp.clip(entries, min=-reach, max=reach).astype(kind)


def setup_inputs(seed: int = 0) -> dict:
    keys = jax.random.split(jax.random.key(seed), 7)
    return {
        "initial_state": normal_values(keys[0], (NP, NP, CHAN, ELY, ELX), 1.0, 6.0, ((3, 16), (4, 8)), jnp.float32),
        "forcing": normal_values(keys[1], (NP, NP, CHAN, ELY, ELX), 1.0, 6.0, ((3, 16), (4, 8)), jnp.float32),
        "jacobian": jnp.clip(jnp.exp(math.log(2.0) - 1.3862944 * jax.random.uniform(keys[2], (NP, NP, ELY, ELX), jnp.float32) ** level_of(keys[2], (NP, NP, ELY, ELX), ((2, 16), (3, 8)), -0.2, 0.2)), 0.5, 2.0),
        "metric": jnp.clip(jnp.exp(math.log(2.0) - 1.3862944 * jax.random.uniform(keys[3], (NP, NP, ELY, ELX), jnp.float32) ** level_of(keys[3], (NP, NP, ELY, ELX), ((2, 16), (3, 8)), -0.2, 0.2)), 0.5, 2.0),
        "viscosity": jnp.clip(jnp.exp(jax.random.uniform(keys[4], (CHAN,), jnp.float32, math.log(0.0001), math.log(0.0006))), 0.0001, 0.0006),
        "element_turns": touch_ends(jax.random.randint(keys[5], (ELY, ELX), 0, 4), jax.random.fold_in(keys[5], 1), 0, 3).astype(jnp.int32),
    }


time_step = 1.0

def lagrange_tables():
    root_five = 1.0 / math.sqrt(5.0)
    points = np.array([-1.0, -root_five, root_five, 1.0])
    weights = np.array([1.0 / 6.0, 5.0 / 6.0, 5.0 / 6.0, 1.0 / 6.0])
    number = points.shape[0]
    products = np.ones(number)
    for row_index in range(number):
        for other_index in range(number):
            if other_index != row_index:
                products[row_index] = products[row_index] * (points[row_index] - points[other_index])
    derivative = np.zeros((number, number))
    for row_index in range(number):
        for column_index in range(number):
            if row_index == column_index:
                derivative[row_index, column_index] = sum((1.0 / (points[row_index] - points[other_index]) for other_index in range(number) if other_index != row_index))
            else:
                derivative[row_index, column_index] = products[row_index] / (products[column_index] * (points[row_index] - points[column_index]))
    return (derivative, weights)

def face_frame(values, element_turns):
    result = values
    turned = values
    for quarter in range(1, 4):
        turned = jnp.rot90(turned, 1, axes=(0, 1))
        result = jnp.where(element_turns == quarter, turned, result)
    return result

def stiffness(nodal_field, derivative, flux_weight):
    highest = lax.Precision.HIGHEST
    along_x = jnp.einsum('ai,jikyx->jakyx', derivative, nodal_field, precision=highest)
    along_y = jnp.einsum('bj,jikyx->bikyx', derivative, nodal_field, precision=highest)
    flux_x = flux_weight[:, :, None] * along_x
    flux_y = flux_weight[:, :, None] * along_y
    part_x = jnp.einsum('ac,jakyx->jckyx', derivative, flux_x, precision=highest)
    part_y = jnp.einsum('bc,bikyx->cikyx', derivative, flux_y, precision=highest)
    return -(part_x + part_y)

def assemble(nodal_field):
    left_nodes = nodal_field[:, 0]
    right_nodes = nodal_field[:, NP - 1]
    new_left = left_nodes + jnp.roll(right_nodes, 1, axis=-1)
    new_right = right_nodes + jnp.roll(left_nodes, -1, axis=-1)
    nodal_field = jnp.concatenate([new_left[:, None], nodal_field[:, 1:NP - 1], new_right[:, None]], axis=1)
    lower_rim = nodal_field[0]
    upper_rim = nodal_field[NP - 1]
    zeros_row = jnp.zeros_like(upper_rim[:, :, :1])
    new_lower = lower_rim + jnp.concatenate([zeros_row, upper_rim[:, :, :-1]], axis=2)
    new_upper = upper_rim + jnp.concatenate([lower_rim[:, :, 1:], zeros_row], axis=2)
    return jnp.concatenate([new_lower[None], nodal_field[1:NP - 1], new_upper[None]], axis=0)

def reference(initial_state, forcing, jacobian, metric, viscosity, element_turns):
    derivative_np, weights_np = lagrange_tables()
    derivative = jnp.asarray(derivative_np, jnp.float32)
    weights = jnp.asarray(weights_np, jnp.float32)
    state_face = face_frame(initial_state, element_turns)
    forcing_face = face_frame(forcing, element_turns)
    jacobian_face = face_frame(jacobian, element_turns)
    metric_face = face_frame(metric, element_turns)
    node_weight = weights[:, None] * weights[None, :]
    local_mass = (node_weight[:, :, None, None] * jacobian_face)[:, :, None]
    flux_weight = node_weight[:, :, None, None] * metric_face
    assembled_mass = assemble(local_mass)
    inverse = 1.0 / assembled_mass
    damping = viscosity[None, None, :, None, None]
    current = state_face
    for section_index in range(SECTIONS):
        factor = time_step / (SECTIONS - section_index)
        first_laplace = assemble(stiffness(current, derivative, flux_weight)) * inverse
        second = assemble(stiffness(first_laplace, derivative, flux_weight)) * inverse
        update = local_mass * (state_face + factor * (forcing_face - damping * second))
        current = assemble(update) * inverse
    return current
```

```python
import functools
import math

import jax
import jax.numpy as jnp
import numpy as np
from jax import lax
from jax.experimental import pallas as pl
from jax.experimental.pallas import tpu as pltpu
from jax.sharding import PartitionSpec as P

NP = 4
SECTIONS = 5
GROUPS = 2
time_step = 1.0
PAIRS = ((0, 1), (0, 2), (0, 3), (1, 2), (1, 3), (2, 3))
NORTH, SOUTH, EAST, WEST, NE, SW, NW, SE = range(8)
STEP = ((0, 1), (0, -1), (1, 0), (-1, 0), (1, 1), (-1, -1), (-1, 1), (1, -1))
MESH = pl.DeviceIdType.MESH


def lagrange_tables():
    root_five = 1.0 / math.sqrt(5.0)
    points = np.array([-1.0, -root_five, root_five, 1.0])
    weights = np.array([1.0 / 6.0, 5.0 / 6.0, 5.0 / 6.0, 1.0 / 6.0])
    number = points.shape[0]
    products = np.ones(number)
    for row in range(number):
        for other in range(number):
            if other != row:
                products[row] = products[row] * (points[row] - points[other])
    derivative = np.zeros((number, number))
    for row in range(number):
        for column in range(number):
            if row == column:
                derivative[row, column] = sum(
                    1.0 / (points[row] - points[other])
                    for other in range(number)
                    if other != row
                )
            else:
                derivative[row, column] = products[row] / (
                    products[column] * (points[row] - points[column])
                )
    return (derivative, weights)


def turned(v):
    return [[v[i][NP - 1 - j] for i in range(NP)] for j in range(NP)]


def face_frame(v, masks):
    result = v
    for mask in masks:
        v = turned(v)
        result = [
            [jnp.where(mask, v[j][i], result[j][i]) for i in range(NP)]
            for j in range(NP)
        ]
    return result


def kernel(
    sizes,
    state_ref,
    forcing_ref,
    jacobian_ref,
    metric_ref,
    turns_ref,
    viscosity_ref,
    out_ref,
    part_ref,
    base_ref,
    tend_ref,
    inverse_ref,
    own_k_ref,
    both_k_ref,
    diagonal_ref,
    mass_ref,
    out_rows,
    out_tiles,
    in_rows,
    in_tiles,
    send_sem,
    recv_sem,
    set_out_rows,
    set_out_tiles,
    set_in_rows,
    set_in_tiles,
    set_send,
    set_recv,
    ini_out_rows,
    ini_out_tiles,
    ini_in_rows,
    ini_in_tiles,
    ini_send,
    ini_recv,
):
    chan, rows, cols, count_x, count_y = sizes
    per = chan // GROUPS
    last_row, last_col = rows - 1, cols - 1
    derivative, weights = lagrange_tables()
    cx = lax.axis_index("gx")
    cy = lax.axis_index("gy")
    lane = lax.broadcasted_iota(jnp.int32, (rows, cols), 1)
    sub = lax.broadcasted_iota(jnp.int32, (rows, cols), 0)
    at_west, at_east = lane == 0, lane == last_col
    at_south, at_north = sub == 0, sub == last_row
    zero = jnp.zeros((rows, cols), jnp.float32)
    there_north = cy < count_y - 1
    there_south = cy > 0

    def device(d):
        dx, dy = STEP[d]
        return (lax.rem(cx + dx + count_x, count_x), cy + dy)

    def for_each(todo):
        for d in (EAST, WEST):
            todo(d)

        @pl.when(there_north)
        def _():
            for d in (NORTH, NE, NW):
                todo(d)

        @pl.when(there_south)
        def _():
            for d in (SOUTH, SE, SW):
                todo(d)

    def copy(bufs, where_out, where_in, d, arriving=False):
        o_rows, o_tiles, i_rows, i_tiles, ssem, rsem = bufs
        slot = d if arriving else d ^ 1
        if d in (NORTH, SOUTH):
            src, dst = o_rows.at[(d,) + where_out], i_rows.at[(slot,) + where_in]
        else:
            src = o_tiles.at[(d - 2,) + where_out]
            dst = i_tiles.at[(slot - 2,) + where_in]
        return pltpu.make_async_remote_copy(
            src_ref=src,
            dst_ref=dst,
            send_sem=ssem.at[(d,) + where_out],
            recv_sem=rsem.at[(slot,) + where_in],
            device_id=device(d),
            device_id_type=MESH,
        )

    def start(bufs, where_out, where_in):
        for_each(lambda d: copy(bufs, where_out, where_in, d).start())

    def finish(bufs, where_out, where_in):
        def todo(d):
            c = copy(bufs, where_out, where_in, d, arriving=True)
            c.wait_recv()
            c.wait_send()

        for_each(todo)

    main = (out_rows, out_tiles, in_rows, in_tiles, send_sem, recv_sem)
    sets = (set_out_rows, set_out_tiles, set_in_rows, set_in_tiles, set_send, set_recv)
    ini = (ini_out_rows, ini_out_tiles, ini_in_rows, ini_in_tiles, ini_send, ini_recv)

    def join_x(a, b):
        return (
            a + jnp.where(at_west, 0.0, pltpu.roll(b, 1, 1)),
            b + jnp.where(at_east, 0.0, pltpu.roll(a, cols - 1, 1)),
        )

    def join_y(a, b):
        return (
            a + jnp.where(at_south, 0.0, pltpu.roll(b, 1, 0)),
            b + jnp.where(at_north, 0.0, pltpu.roll(a, rows - 1, 0)),
        )

    def join(s):
        s = [list(r) for r in s]
        for j in range(NP):
            s[j][0], s[j][3] = join_x(s[j][0], s[j][3])
        for i in range(NP):
            s[0][i], s[3][i] = join_y(s[0][i], s[3][i])
        return s

    def line(v, k):
        p = [k[n] * (v[b] - v[a]) for n, (a, b) in enumerate(PAIRS)]
        return (
            p[0] + p[1] + p[2],
            p[3] + p[4] - p[0],
            p[5] - p[1] - p[3],
            -(p[2] + p[4] + p[5]),
        )

    def stiff(v, k_ref):
        s = [[None] * NP for _ in range(NP)]
        for j in range(NP):
            got = line(v[j], [k_ref[j * 6 + n] for n in range(6)])
            for i in range(NP):
                s[j][i] = got[i]
        for i in range(NP):
            got = line(
                [v[j][i] for j in range(NP)],
                [k_ref[24 + i * 6 + n] for n in range(6)],
            )
            for j in range(NP):
                s[j][i] = s[j][i] + got[j]
        return join(s)

    def from_inside(w):
        rx = [[None] * NP for _ in range(NP)]
        ry = [[None] * NP for _ in range(NP)]
        for j in range(NP):
            k = [both_k_ref[j * 6 + n] for n in range(6)]
            rx[j][0] = k[0] * w[j][1] + k[1] * w[j][2] + k[2] * w[j][3]
            rx[j][3] = k[2] * w[j][0] + k[4] * w[j][1] + k[5] * w[j][2]
        for i in range(NP):
            k = [both_k_ref[24 + i * 6 + n] for n in range(6)]
            ry[0][i] = k[0] * w[1][i] + k[1] * w[2][i] + k[2] * w[3][i]
            ry[3][i] = k[2] * w[0][i] + k[4] * w[1][i] + k[5] * w[2][i]
        return joined_edges(rx, ry)

    def joined_edges(rx, ry):
        for i in (0, 3):
            rx[0][i], rx[3][i] = join_y(rx[0][i], rx[3][i])
        for j in (0, 3):
            ry[j][0], ry[j][3] = join_x(ry[j][0], ry[j][3])
        return rx, ry

    def load(ref, c):
        return [[ref[j, i, c] for i in range(NP)] for j in range(NP)]

    def store(ref, c, v):
        for j in range(NP):
            for i in range(NP):
                ref[j, i, c] = v[j][i]

    def times(v, ref):
        return [[v[j][i] * ref[j * NP + i] for i in range(NP)] for j in range(NP)]

    def lay_rows(ref, where, k, top, bottom):
        ref[(NORTH,) + where + (slice(k, k + 1), slice(None))] = top[last_row:, :]
        ref[(SOUTH,) + where + (slice(k, k + 1), slice(None))] = bottom[0:1, :]

    def lay_lane(tiles, n, right, left, corner):
        here = lane == n
        from_right = lax.rem(n + 1, cols)

        def put(d, v, shift):
            tiles[d - 2] = jnp.where(here, pltpu.roll(v, shift, 1), tiles[d - 2])

        if right is not None:
            put(EAST, right, from_right)
            put(WEST, left, n)
        if corner is not None:
            put(NE, corner[0], from_right)
            put(SW, corner[1], n)
            put(NW, corner[2], n)
            put(SE, corner[3], from_right)

    def emit(refs, where, c, tiles, fields):
        tiles = list(tiles)
        for q, (vx, vy, corner) in enumerate(fields):
            for i in range(NP):
                lay_rows(refs[0], where + (c,), q * NP + i, vy[3][i], vy[0][i])
            for j in range(NP):
                n = (q * NP + j) * per + c
                lay_lane(tiles, n, vx[j][3], vx[j][0], None)
            lay_lane(tiles, q * per + c, None, None, corner)
        return tuple(tiles)

    def corners_of(v):
        return (v[3][3], v[0][0], v[3][0], v[0][3])

    def row(ref, where, k):
        return jnp.broadcast_to(
            ref[where + (slice(k, k + 1), slice(None))], (rows, cols)
        )

    def in_tiles_of(ref, where):
        got = [ref[(d - 2,) + where] for d in range(2, 8)]
        for d in (NE, NW):
            got[d - 2] = pltpu.roll(got[d - 2], rows - 1, 0)
        for d in (SE, SW):
            got[d - 2] = pltpu.roll(got[d - 2], 1, 0)
        return got

    def add_in(v, ref, where, c, got, q):
        v = [list(r) for r in v]

        def from_lane(d, n):
            if d in (EAST, NE, SE):
                return pltpu.roll(got[d - 2], last_col - n, 1)
            return pltpu.roll(got[d - 2], lax.rem(cols - n, cols), 1)

        for i in range(NP):
            k = q * NP + i
            v[3][i] = v[3][i] + jnp.where(at_north, row(ref, (NORTH,) + where + (c,), k), 0.0)
            v[0][i] = v[0][i] + jnp.where(at_south, row(ref, (SOUTH,) + where + (c,), k), 0.0)
        for j in range(NP):
            n = (q * NP + j) * per + c
            v[j][3] = v[j][3] + jnp.where(at_east, from_lane(EAST, n), 0.0)
            v[j][0] = v[j][0] + jnp.where(at_west, from_lane(WEST, n), 0.0)
        n = q * per + c
        for d, j, i, m in (
            (NE, 3, 3, at_north & at_east),
            (SW, 0, 0, at_south & at_west),
            (NW, 3, 0, at_north & at_west),
            (SE, 0, 3, at_south & at_east),
        ):
            v[j][i] = v[j][i] + jnp.where(m, from_lane(d, n), 0.0)
        return v

    def keep_tiles(ref, where, tiles):
        for d in range(2, 8):
            ref[(d - 2,) + where] = tiles[d - 2]

    in_rows[...] = jnp.zeros_like(in_rows)
    in_tiles[...] = jnp.zeros_like(in_tiles)
    set_in_rows[...] = jnp.zeros_like(set_in_rows)
    set_in_tiles[...] = jnp.zeros_like(set_in_tiles)
    ini_in_rows[...] = jnp.zeros_like(ini_in_rows)
    ini_in_tiles[...] = jnp.zeros_like(ini_in_tiles)
    barrier = pltpu.get_barrier_semaphore()
    for_each(
        lambda d: pl.semaphore_signal(
            barrier, inc=1, device_id=device(d), device_id_type=MESH
        )
    )
    peers = 2 + 3 * there_north.astype(jnp.int32) + 3 * there_south.astype(jnp.int32)
    pl.semaphore_wait(barrier, peers)

    turns = turns_ref[...]
    masks = [turns == quarter for quarter in range(1, 4)]
    jacobian = face_frame(
        [[jacobian_ref[j, i] for i in range(NP)] for j in range(NP)], masks
    )
    metric = face_frame(
        [[metric_ref[j, i] for i in range(NP)] for j in range(NP)], masks
    )
    mass = [
        [float(weights[j] * weights[i]) * jacobian[j][i] for i in range(NP)]
        for j in range(NP)
    ]
    flux = [
        [float(weights[j] * weights[i]) * metric[j][i] for i in range(NP)]
        for j in range(NP)
    ]
    for j in range(NP):
        for i in range(NP):
            mass_ref[j * NP + i] = mass[j][i]

    def coefficients(f):
        return [
            sum(float(-derivative[n, a] * derivative[n, b]) * f[n] for n in range(NP))
            for a, b in PAIRS
        ]

    kx = [coefficients(flux[j]) for j in range(NP)]
    ky = [coefficients([flux[j][i] for j in range(NP)]) for i in range(NP)]
    for m in range(NP):
        for n in range(6):
            own_k_ref[m * 6 + n] = kx[m][n]
            own_k_ref[24 + m * 6 + n] = ky[m][n]
    first = lambda k: k[0] + k[1] + k[2]
    final = lambda k: k[2] + k[4] + k[5]
    dx = [[first(kx[j]), None, None, final(kx[j])] for j in range(NP)]
    dy = [[None] * NP for _ in range(NP)]
    for i in range(NP):
        dy[0][i], dy[3][i] = first(ky[i]), final(ky[i])
    dx, dy = joined_edges(dx, dy)
    local = join(mass)
    tiles = [zero] * 6
    for n in range(NP):
        lay_rows(ini_out_rows, (0,), n, local[3][n], local[0][n])
        lay_rows(ini_out_rows, (0,), 4 + n, dy[3][n], dy[0][n])
        lay_lane(tiles, n, local[n][3], local[n][0], None)
        lay_lane(tiles, 4 + n, dx[n][3], dx[n][0], None)
    for n in range(6):
        lay_rows(ini_out_rows, (1,), n, kx[3][n], kx[0][n])
        lay_lane(tiles, 8 + n, ky[3][n], ky[0][n], None)
    lay_lane(tiles, 0, None, None, corners_of(local))
    both = [[None] * NP for _ in range(NP)]
    for j in (0, 3):
        for i in (0, 3):
            both[j][i] = dx[j][i] + dy[j][i]
    lay_lane(tiles, 1, None, None, corners_of(both))
    for n in (6, 7):
        lay_rows(ini_out_rows, (1,), n, zero, zero)
    keep_tiles(ini_out_tiles, (), tiles)
    start(ini, (), ())

    def enter_group(g):
        def enter(c, tiles):
            ch = g * per + c
            state = face_frame(load(state_ref, ch), masks)
            forcing = face_frame(load(forcing_ref, ch), masks)
            base = join(times(state, mass_ref))
            tend = join(times(forcing, mass_ref))
            store(base_ref, ch, base)
            store(tend_ref, ch, tend)
            tiles = emit(
                sets,
                (g,),
                c,
                tiles,
                ((base, base, corners_of(base)), (tend, tend, corners_of(tend))),
            )
            store(part_ref, ch, stiff(state, own_k_ref))
            return tiles

        tiles = lax.fori_loop(0, per, enter, (zero,) * 6)
        keep_tiles(set_out_tiles, (g,), tiles)
        start(sets, (g,), (g,))

    pl.loop(0, GROUPS)(enter_group)

    finish(ini, (), ())
    got = in_tiles_of(ini_in_tiles, ())

    def lane_of(d, n):
        to = last_col if d in (EAST, NE, SE) else 0
        return pltpu.roll(got[d - 2], (to - n) % cols, 1)

    def north(block, k):
        return jnp.where(at_north, row(ini_in_rows, (NORTH, block), k), 0.0)

    def south(block, k):
        return jnp.where(at_south, row(ini_in_rows, (SOUTH, block), k), 0.0)

    def east(n):
        return jnp.where(at_east, lane_of(EAST, n), 0.0)

    def west(n):
        return jnp.where(at_west, lane_of(WEST, n), 0.0)

    def with_neighbours(v, first_k, corner_n):
        v = [list(r) for r in v]
        for i in range(NP):
            v[3][i] = v[3][i] + north(0, first_k + i)
            v[0][i] = v[0][i] + south(0, first_k + i)
        for j in range(NP):
            v[j][3] = v[j][3] + east(first_k + j)
            v[j][0] = v[j][0] + west(first_k + j)
        for d, j, i, m in (
            (NE, 3, 3, at_north & at_east),
            (SW, 0, 0, at_south & at_west),
            (NW, 3, 0, at_north & at_west),
            (SE, 0, 3, at_south & at_east),
        ):
            v[j][i] = v[j][i] + jnp.where(m, lane_of(d, corner_n), 0.0)
        return v

    assembled = with_neighbours(local, 0, 0)
    diagonal = with_neighbours([[zero] * NP for _ in range(NP)], 4, 1)
    for j in range(NP):
        for i in range(NP):
            inverse_ref[j * NP + i] = 1.0 / assembled[j][i]
            diagonal_ref[j * NP + i] = diagonal[j][i]
    for m in range(NP):
        for n in range(6):
            x, y = kx[m][n], ky[m][n]
            if m == 0:
                x, y = x + south(1, n), y + west(8 + n)
            if m == 3:
                x, y = x + north(1, n), y + east(8 + n)
            both_k_ref[m * 6 + n] = x
            both_k_ref[24 + m * 6 + n] = y

    def emit_main(g, c, tiles, s):
        rx, ry = from_inside(times(s, inverse_ref))
        corner = tuple(
            rx[j][i] + ry[j][i] for j, i in ((3, 3), (0, 0), (3, 0), (0, 3))
        )
        return emit(main, (g,), c, tiles, ((s, s, corners_of(s)), (rx, ry, corner)))

    def send_group(g):
        def send(c, tiles):
            return emit_main(g, c, tiles, load(part_ref, g * per + c))

        tiles = lax.fori_loop(0, per, send, (zero,) * 6)
        keep_tiles(out_tiles, (g,), tiles)
        start(main, (g,), (0, g))

    pl.loop(0, GROUPS)(send_group)

    def settle_group(g):
        finish(sets, (g,), (g,))
        got = in_tiles_of(set_in_tiles, (g,))

        def settle(c, carry):
            ch = g * per + c
            for q, ref in enumerate((base_ref, tend_ref)):
                v = add_in(load(ref, ch), set_in_rows, (g,), c, got, q)
                store(ref, ch, times(v, inverse_ref))
            return carry

        lax.fori_loop(0, per, settle, 0)

    pl.loop(0, GROUPS)(settle_group)

    def advance(ch, c, g, parity, got, factor):
        where = (parity, g)
        s = add_in(load(part_ref, ch), in_rows, where, c, got, 0)
        w = times(s, inverse_ref)
        t = add_in(stiff(w, both_k_ref), in_rows, where, c, got, 1)
        scale = factor * viscosity_ref[ch]
        for j in range(NP):
            for i in range(NP):
                if j in (0, 3) or i in (0, 3):
                    t[j][i] = t[j][i] - diagonal_ref[j * NP + i] * w[j][i]
        return [
            [
                base_ref[j, i, ch]
                + (
                    factor * tend_ref[j, i, ch]
                    - scale * (t[j][i] * inverse_ref[j * NP + i])
                )
                for i in range(NP)
            ]
            for j in range(NP)
        ]

    def section_group(step):
        section, g = step // GROUPS, lax.rem(step, GROUPS)
        parity = lax.rem(section, 2)
        factor = jnp.float32(time_step / SECTIONS)
        for m in range(1, SECTIONS - 1):
            factor = jnp.where(
                section == m, jnp.float32(time_step / (SECTIONS - m)), factor
            )
        finish(main, (g,), (parity, g))
        got = in_tiles_of(in_tiles, (parity, g))

        def body(c, tiles):
            ch = g * per + c
            u = advance(ch, c, g, parity, got, factor)
            s = stiff(u, own_k_ref)
            store(part_ref, ch, s)
            return emit_main(g, c, tiles, s)

        tiles = lax.fori_loop(0, per, body, (zero,) * 6)
        keep_tiles(out_tiles, (g,), tiles)
        start(main, (g,), (1 - parity, g))

    pl.loop(0, (SECTIONS - 1) * GROUPS)(section_group)

    def last_group(g):
        parity = (SECTIONS - 1) % 2
        finish(main, (g,), (parity, g))
        got = in_tiles_of(in_tiles, (parity, g))

        def body(c, carry):
            ch = g * per + c
            store(out_ref, ch, advance(ch, c, g, parity, got, jnp.float32(time_step)))
            return carry

        lax.fori_loop(0, per, body, 0)

    pl.loop(0, GROUPS)(last_group)


def on_device(
    counts, initial_state, forcing, jacobian, metric, viscosity, element_turns
):
    np0, np1, chan, rows, cols = initial_state.shape
    per = chan // GROUPS
    f32 = jnp.float32
    field = pltpu.VMEM((NP, NP, chan, rows, cols), f32)
    vmem = pl.BlockSpec(memory_space=pltpu.VMEM)

    def buffers(out_lead, in_lead, tiles_per_rows):
        dma = pltpu.SemaphoreType.DMA
        return [
            pltpu.VMEM((2,) + out_lead + (tiles_per_rows, rows, cols), f32),
            pltpu.VMEM((6,) + out_lead + (rows, cols), f32),
            pltpu.VMEM((2,) + in_lead + (tiles_per_rows, rows, cols), f32),
            pltpu.VMEM((6,) + in_lead + (rows, cols), f32),
            dma((8,) + out_lead),
            dma((8,) + in_lead),
        ]

    return pl.pallas_call(
        functools.partial(kernel, (chan, rows, cols) + counts),
        out_shape=jax.ShapeDtypeStruct(initial_state.shape, f32),
        in_specs=[vmem] * 5 + [pl.BlockSpec(memory_space=pltpu.SMEM)],
        out_specs=vmem,
        scratch_shapes=[
            field,
            field,
            field,
            pltpu.VMEM((16, rows, cols), f32),
            pltpu.VMEM((48, rows, cols), f32),
            pltpu.VMEM((48, rows, cols), f32),
            pltpu.VMEM((16, rows, cols), f32),
            pltpu.VMEM((16, rows, cols), f32),
        ]
        + buffers((GROUPS,), (2, GROUPS), per)
        + buffers((GROUPS,), (GROUPS,), per)
        + buffers((), (), 2),
        compiler_params=pltpu.CompilerParams(
            collective_id=0, has_side_effects=True, vmem_limit_bytes=48 * 2**20
        ),
    )(initial_state, forcing, jacobian, metric, element_turns, viscosity)


def solution(mesh):
    placed = (
        P(None, None, None, "gy", "gx"),
        P(None, None, None, "gy", "gx"),
        P(None, None, "gy", "gx"),
        P(None, None, "gy", "gx"),
        P(),
        P("gy", "gx"),
    )
    return jax.shard_map(
        functools.partial(on_device, (mesh.shape["gx"], mesh.shape["gy"])),
        mesh=mesh,
        in_specs=placed,
        out_specs=P(None, None, None, "gy", "gx"),
        check_vma=False,
    )
```

```python
import functools
import math

import jax
import jax.numpy as jnp
import numpy as np
from jax import lax
from jax.experimental import pallas as pl
from jax.experimental.pallas import tpu as pltpu
from jax.sharding import PartitionSpec as P

NP = 4
SECTIONS = 5
GROUPS = 2
UNROLL = 4
time_step = 1.0
PAIRS = ((0, 1), (0, 2), (0, 3), (1, 2), (1, 3), (2, 3))
NORTH, SOUTH, EAST, WEST, NE, SW, NW, SE = range(8)
STEP = ((0, 1), (0, -1), (1, 0), (-1, 0), (1, 1), (-1, -1), (-1, 1), (1, -1))
MESH = pl.DeviceIdType.MESH


def lagrange_tables():
    root_five = 1.0 / math.sqrt(5.0)
    points = np.array([-1.0, -root_five, root_five, 1.0])
    weights = np.array([1.0 / 6.0, 5.0 / 6.0, 5.0 / 6.0, 1.0 / 6.0])
    number = points.shape[0]
    products = np.ones(number)
    for row in range(number):
        for other in range(number):
            if other != row:
                products[row] = products[row] * (points[row] - points[other])
    derivative = np.zeros((number, number))
    for row in range(number):
        for column in range(number):
            if row == column:
                derivative[row, column] = sum(
                    1.0 / (points[row] - points[other])
                    for other in range(number)
                    if other != row
                )
            else:
                derivative[row, column] = products[row] / (
                    products[column] * (points[row] - points[column])
                )
    return (derivative, weights)


def turned(v):
    return [[v[i][NP - 1 - j] for i in range(NP)] for j in range(NP)]


def face_frame(v, masks):
    result = v
    for mask in masks:
        v = turned(v)
        result = [
            [jnp.where(mask, v[j][i], result[j][i]) for i in range(NP)]
            for j in range(NP)
        ]
    return result


def kernel(
    sizes,
    state_ref,
    forcing_ref,
    jacobian_ref,
    metric_ref,
    turns_ref,
    viscosity_ref,
    out_ref,
    part_ref,
    base_ref,
    tend_ref,
    inverse_ref,
    own_k_ref,
    both_k_ref,
    diagonal_ref,
    mass_ref,
    out_rows,
    out_tiles,
    in_rows,
    in_tiles,
    send_sem,
    recv_sem,
    set_out_rows,
    set_out_tiles,
    set_in_rows,
    set_in_tiles,
    set_send,
    set_recv,
    ini_out_rows,
    ini_out_tiles,
    ini_in_rows,
    ini_in_tiles,
    ini_send,
    ini_recv,
):
    chan, rows, cols, count_x, count_y = sizes
    per = chan // GROUPS
    last_row, last_col = rows - 1, cols - 1
    derivative, weights = lagrange_tables()
    cx = lax.axis_index("gx")
    cy = lax.axis_index("gy")
    lane = lax.broadcasted_iota(jnp.int32, (rows, cols), 1)
    sub = lax.broadcasted_iota(jnp.int32, (rows, cols), 0)
    at_west, at_east = lane == 0, lane == last_col
    at_south, at_north = sub == 0, sub == last_row
    zero = jnp.zeros((rows, cols), jnp.float32)
    there_north = cy < count_y - 1
    there_south = cy > 0

    def device(d):
        dx, dy = STEP[d]
        return (lax.rem(cx + dx + count_x, count_x), cy + dy)

    def for_each(todo):
        for d in (EAST, WEST):
            todo(d)

        @pl.when(there_north)
        def _():
            for d in (NORTH, NE, NW):
                todo(d)

        @pl.when(there_south)
        def _():
            for d in (SOUTH, SE, SW):
                todo(d)

    def copy(bufs, where_out, where_in, d, arriving=False):
        o_rows, o_tiles, i_rows, i_tiles, ssem, rsem = bufs
        slot = d if arriving else d ^ 1
        if d in (NORTH, SOUTH):
            src, dst = o_rows.at[(d,) + where_out], i_rows.at[(slot,) + where_in]
        else:
            src = o_tiles.at[(d - 2,) + where_out]
            dst = i_tiles.at[(slot - 2,) + where_in]
        return pltpu.make_async_remote_copy(
            src_ref=src,
            dst_ref=dst,
            send_sem=ssem.at[(d,) + where_out],
            recv_sem=rsem.at[(slot,) + where_in],
            device_id=device(d),
            device_id_type=MESH,
        )

    def start(bufs, where_out, where_in):
        for_each(lambda d: copy(bufs, where_out, where_in, d).start())

    def finish(bufs, where_out, where_in):
        def todo(d):
            c = copy(bufs, where_out, where_in, d, arriving=True)
            c.wait_recv()
            c.wait_send()

        for_each(todo)

    main = (out_rows, out_tiles, in_rows, in_tiles, send_sem, recv_sem)
    sets = (set_out_rows, set_out_tiles, set_in_rows, set_in_tiles, set_send, set_recv)
    ini = (ini_out_rows, ini_out_tiles, ini_in_rows, ini_in_tiles, ini_send, ini_recv)

    def join_x(a, b):
        return (
            a + jnp.where(at_west, 0.0, pltpu.roll(b, 1, 1)),
            b + jnp.where(at_east, 0.0, pltpu.roll(a, cols - 1, 1)),
        )

    def join_y(a, b):
        return (
            a + jnp.where(at_south, 0.0, pltpu.roll(b, 1, 0)),
            b + jnp.where(at_north, 0.0, pltpu.roll(a, rows - 1, 0)),
        )

    def join(s):
        s = [list(r) for r in s]
        for j in range(NP):
            s[j][0], s[j][3] = join_x(s[j][0], s[j][3])
        for i in range(NP):
            s[0][i], s[3][i] = join_y(s[0][i], s[3][i])
        return s

    def line(v, k):
        p = [k[n] * (v[b] - v[a]) for n, (a, b) in enumerate(PAIRS)]
        return (
            p[0] + p[1] + p[2],
            p[3] + p[4] - p[0],
            p[5] - p[1] - p[3],
            -(p[2] + p[4] + p[5]),
        )

    def stiff(v, k_ref):
        s = [[None] * NP for _ in range(NP)]
        for j in range(NP):
            got = line(v[j], [k_ref[j * 6 + n] for n in range(6)])
            for i in range(NP):
                s[j][i] = got[i]
        for i in range(NP):
            got = line(
                [v[j][i] for j in range(NP)],
                [k_ref[24 + i * 6 + n] for n in range(6)],
            )
            for j in range(NP):
                s[j][i] = s[j][i] + got[j]
        return join(s)

    def from_inside(w):
        rx = [[None] * NP for _ in range(NP)]
        ry = [[None] * NP for _ in range(NP)]
        for j in range(NP):
            k = [both_k_ref[j * 6 + n] for n in range(6)]
            rx[j][0] = k[0] * w[j][1] + k[1] * w[j][2] + k[2] * w[j][3]
            rx[j][3] = k[2] * w[j][0] + k[4] * w[j][1] + k[5] * w[j][2]
        for i in range(NP):
            k = [both_k_ref[24 + i * 6 + n] for n in range(6)]
            ry[0][i] = k[0] * w[1][i] + k[1] * w[2][i] + k[2] * w[3][i]
            ry[3][i] = k[2] * w[0][i] + k[4] * w[1][i] + k[5] * w[2][i]
        return joined_edges(rx, ry)

    def joined_edges(rx, ry):
        for i in (0, 3):
            rx[0][i], rx[3][i] = join_y(rx[0][i], rx[3][i])
        for j in (0, 3):
            ry[j][0], ry[j][3] = join_x(ry[j][0], ry[j][3])
        return rx, ry

    def load(ref, c):
        return [[ref[j, i, c] for i in range(NP)] for j in range(NP)]

    def store(ref, c, v):
        for j in range(NP):
            for i in range(NP):
                ref[j, i, c] = v[j][i]

    def times(v, ref):
        return [[v[j][i] * ref[j * NP + i] for i in range(NP)] for j in range(NP)]

    def lay_rows(ref, where, k, top, bottom):
        ref[(NORTH,) + where + (slice(k, k + 1), slice(None))] = top[last_row:, :]
        ref[(SOUTH,) + where + (slice(k, k + 1), slice(None))] = bottom[0:1, :]

    def lay_lane(tiles, n, right, left, corner):
        here = lane == n
        from_right = lax.rem(n + 1, cols)

        def put(d, v, shift):
            tiles[d - 2] = jnp.where(here, pltpu.roll(v, shift, 1), tiles[d - 2])

        if right is not None:
            put(EAST, right, from_right)
            put(WEST, left, n)
        if corner is not None:
            put(NE, corner[0], from_right)
            put(SW, corner[1], n)
            put(NW, corner[2], n)
            put(SE, corner[3], from_right)

    def emit(refs, where, c, tiles, fields):
        tiles = list(tiles)
        for q, (vx, vy, corner) in enumerate(fields):
            for i in range(NP):
                lay_rows(refs[0], where + (c,), q * NP + i, vy[3][i], vy[0][i])
            for j in range(NP):
                n = (q * NP + j) * per + c
                lay_lane(tiles, n, vx[j][3], vx[j][0], None)
            lay_lane(tiles, q * per + c, None, None, corner)
        return tuple(tiles)

    def corners_of(v):
        return (v[3][3], v[0][0], v[3][0], v[0][3])

    def row(ref, where, k):
        return jnp.broadcast_to(
            ref[where + (slice(k, k + 1), slice(None))], (rows, cols)
        )

    def in_tiles_of(ref, where):
        got = [ref[(d - 2,) + where] for d in range(2, 8)]
        for d in (NE, NW):
            got[d - 2] = pltpu.roll(got[d - 2], rows - 1, 0)
        for d in (SE, SW):
            got[d - 2] = pltpu.roll(got[d - 2], 1, 0)
        return got

    def add_in(v, ref, where, c, got, q):
        v = [list(r) for r in v]

        def from_lane(d, n):
            if d in (EAST, NE, SE):
                return pltpu.roll(got[d - 2], last_col - n, 1)
            return pltpu.roll(got[d - 2], lax.rem(cols - n, cols), 1)

        for i in range(NP):
            k = q * NP + i
            v[3][i] = v[3][i] + jnp.where(at_north, row(ref, (NORTH,) + where + (c,), k), 0.0)
            v[0][i] = v[0][i] + jnp.where(at_south, row(ref, (SOUTH,) + where + (c,), k), 0.0)
        for j in range(NP):
            n = (q * NP + j) * per + c
            v[j][3] = v[j][3] + jnp.where(at_east, from_lane(EAST, n), 0.0)
            v[j][0] = v[j][0] + jnp.where(at_west, from_lane(WEST, n), 0.0)
        n = q * per + c
        for d, j, i, m in (
            (NE, 3, 3, at_north & at_east),
            (SW, 0, 0, at_south & at_west),
            (NW, 3, 0, at_north & at_west),
            (SE, 0, 3, at_south & at_east),
        ):
            v[j][i] = v[j][i] + jnp.where(m, from_lane(d, n), 0.0)
        return v

    def keep_tiles(ref, where, tiles):
        for d in range(2, 8):
            ref[(d - 2,) + where] = tiles[d - 2]

    in_rows[...] = jnp.zeros_like(in_rows)
    in_tiles[...] = jnp.zeros_like(in_tiles)
    set_in_rows[...] = jnp.zeros_like(set_in_rows)
    set_in_tiles[...] = jnp.zeros_like(set_in_tiles)
    ini_in_rows[...] = jnp.zeros_like(ini_in_rows)
    ini_in_tiles[...] = jnp.zeros_like(ini_in_tiles)
    barrier = pltpu.get_barrier_semaphore()
    for_each(
        lambda d: pl.semaphore_signal(
            barrier, inc=1, device_id=device(d), device_id_type=MESH
        )
    )
    peers = 2 + 3 * there_north.astype(jnp.int32) + 3 * there_south.astype(jnp.int32)
    pl.semaphore_wait(barrier, peers)

    turns = turns_ref[...]
    masks = [turns == quarter for quarter in range(1, 4)]
    jacobian = face_frame(
        [[jacobian_ref[j, i] for i in range(NP)] for j in range(NP)], masks
    )
    metric = face_frame(
        [[metric_ref[j, i] for i in range(NP)] for j in range(NP)], masks
    )
    mass = [
        [float(weights[j] * weights[i]) * jacobian[j][i] for i in range(NP)]
        for j in range(NP)
    ]
    flux = [
        [float(weights[j] * weights[i]) * metric[j][i] for i in range(NP)]
        for j in range(NP)
    ]
    for j in range(NP):
        for i in range(NP):
            mass_ref[j * NP + i] = mass[j][i]

    def coefficients(f):
        return [
            sum(float(-derivative[n, a] * derivative[n, b]) * f[n] for n in range(NP))
            for a, b in PAIRS
        ]

    kx = [coefficients(flux[j]) for j in range(NP)]
    ky = [coefficients([flux[j][i] for j in range(NP)]) for i in range(NP)]
    for m in range(NP):
        for n in range(6):
            own_k_ref[m * 6 + n] = kx[m][n]
            own_k_ref[24 + m * 6 + n] = ky[m][n]
    first = lambda k: k[0] + k[1] + k[2]
    final = lambda k: k[2] + k[4] + k[5]
    dx = [[first(kx[j]), None, None, final(kx[j])] for j in range(NP)]
    dy = [[None] * NP for _ in range(NP)]
    for i in range(NP):
        dy[0][i], dy[3][i] = first(ky[i]), final(ky[i])
    dx, dy = joined_edges(dx, dy)
    local = join(mass)
    tiles = [zero] * 6
    for n in range(NP):
        lay_rows(ini_out_rows, (0,), n, local[3][n], local[0][n])
        lay_rows(ini_out_rows, (0,), 4 + n, dy[3][n], dy[0][n])
        lay_lane(tiles, n, local[n][3], local[n][0], None)
        lay_lane(tiles, 4 + n, dx[n][3], dx[n][0], None)
    for n in range(6):
        lay_rows(ini_out_rows, (1,), n, kx[3][n], kx[0][n])
        lay_lane(tiles, 8 + n, ky[3][n], ky[0][n], None)
    lay_lane(tiles, 0, None, None, corners_of(local))
    both = [[None] * NP for _ in range(NP)]
    for j in (0, 3):
        for i in (0, 3):
            both[j][i] = dx[j][i] + dy[j][i]
    lay_lane(tiles, 1, None, None, corners_of(both))
    for n in (6, 7):
        lay_rows(ini_out_rows, (1,), n, zero, zero)
    keep_tiles(ini_out_tiles, (), tiles)
    start(ini, (), ())

    def enter_group(g):
        def enter(c, tiles):
            ch = g * per + c
            state = face_frame(load(state_ref, ch), masks)
            forcing = face_frame(load(forcing_ref, ch), masks)
            base = join(times(state, mass_ref))
            tend = join(times(forcing, mass_ref))
            store(base_ref, ch, base)
            store(tend_ref, ch, tend)
            tiles = emit(
                sets,
                (g,),
                c,
                tiles,
                ((base, base, corners_of(base)), (tend, tend, corners_of(tend))),
            )
            store(part_ref, ch, stiff(state, own_k_ref))
            return tiles

        tiles = lax.fori_loop(0, per, enter, (zero,) * 6, unroll=UNROLL)
        keep_tiles(set_out_tiles, (g,), tiles)
        start(sets, (g,), (g,))

    pl.loop(0, GROUPS)(enter_group)

    finish(ini, (), ())
    got = in_tiles_of(ini_in_tiles, ())

    def lane_of(d, n):
        to = last_col if d in (EAST, NE, SE) else 0
        return pltpu.roll(got[d - 2], (to - n) % cols, 1)

    def north(block, k):
        return jnp.where(at_north, row(ini_in_rows, (NORTH, block), k), 0.0)

    def south(block, k):
        return jnp.where(at_south, row(ini_in_rows, (SOUTH, block), k), 0.0)

    def east(n):
        return jnp.where(at_east, lane_of(EAST, n), 0.0)

    def west(n):
        return jnp.where(at_west, lane_of(WEST, n), 0.0)

    def with_neighbours(v, first_k, corner_n):
        v = [list(r) for r in v]
        for i in range(NP):
            v[3][i] = v[3][i] + north(0, first_k + i)
            v[0][i] = v[0][i] + south(0, first_k + i)
        for j in range(NP):
            v[j][3] = v[j][3] + east(first_k + j)
            v[j][0] = v[j][0] + west(first_k + j)
        for d, j, i, m in (
            (NE, 3, 3, at_north & at_east),
            (SW, 0, 0, at_south & at_west),
            (NW, 3, 0, at_north & at_west),
            (SE, 0, 3, at_south & at_east),
        ):
            v[j][i] = v[j][i] + jnp.where(m, lane_of(d, corner_n), 0.0)
        return v

    assembled = with_neighbours(local, 0, 0)
    diagonal = with_neighbours([[zero] * NP for _ in range(NP)], 4, 1)
    for j in range(NP):
        for i in range(NP):
            inverse_ref[j * NP + i] = 1.0 / assembled[j][i]
            diagonal_ref[j * NP + i] = diagonal[j][i]
    for m in range(NP):
        for n in range(6):
            x, y = kx[m][n], ky[m][n]
            if m == 0:
                x, y = x + south(1, n), y + west(8 + n)
            if m == 3:
                x, y = x + north(1, n), y + east(8 + n)
            both_k_ref[m * 6 + n] = x
            both_k_ref[24 + m * 6 + n] = y

    def emit_main(g, c, tiles, s):
        rx, ry = from_inside(times(s, inverse_ref))
        corner = tuple(
            rx[j][i] + ry[j][i] for j, i in ((3, 3), (0, 0), (3, 0), (0, 3))
        )
        return emit(main, (g,), c, tiles, ((s, s, corners_of(s)), (rx, ry, corner)))

    def send_group(g):
        def send(c, tiles):
            return emit_main(g, c, tiles, load(part_ref, g * per + c))

        tiles = lax.fori_loop(0, per, send, (zero,) * 6, unroll=UNROLL)
        keep_tiles(out_tiles, (g,), tiles)
        start(main, (g,), (0, g))

    pl.loop(0, GROUPS)(send_group)

    def settle_group(g):
        finish(sets, (g,), (g,))
        got = in_tiles_of(set_in_tiles, (g,))

        def settle(c, carry):
            ch = g * per + c
            for q, ref in enumerate((base_ref, tend_ref)):
                v = add_in(load(ref, ch), set_in_rows, (g,), c, got, q)
                store(ref, ch, times(v, inverse_ref))
            return carry

        lax.fori_loop(0, per, settle, 0, unroll=UNROLL)

    pl.loop(0, GROUPS)(settle_group)

    def advance(ch, c, g, parity, got, factor):
        where = (parity, g)
        s = add_in(load(part_ref, ch), in_rows, where, c, got, 0)
        w = times(s, inverse_ref)
        t = add_in(stiff(w, both_k_ref), in_rows, where, c, got, 1)
        scale = factor * viscosity_ref[ch]
        for j in range(NP):
            for i in range(NP):
                if j in (0, 3) or i in (0, 3):
                    t[j][i] = t[j][i] - diagonal_ref[j * NP + i] * w[j][i]
        return [
            [
                base_ref[j, i, ch]
                + (
                    factor * tend_ref[j, i, ch]
                    - scale * (t[j][i] * inverse_ref[j * NP + i])
                )
                for i in range(NP)
            ]
            for j in range(NP)
        ]

    def section_group(step):
        section, g = step // GROUPS, lax.rem(step, GROUPS)
        parity = lax.rem(section, 2)
        factor = jnp.float32(time_step / SECTIONS)
        for m in range(1, SECTIONS - 1):
            factor = jnp.where(
                section == m, jnp.float32(time_step / (SECTIONS - m)), factor
            )
        finish(main, (g,), (parity, g))
        got = in_tiles_of(in_tiles, (parity, g))

        def body(c, tiles):
            ch = g * per + c
            u = advance(ch, c, g, parity, got, factor)
            s = stiff(u, own_k_ref)
            store(part_ref, ch, s)
            return emit_main(g, c, tiles, s)

        tiles = lax.fori_loop(0, per, body, (zero,) * 6, unroll=UNROLL)
        keep_tiles(out_tiles, (g,), tiles)
        start(main, (g,), (1 - parity, g))

    pl.loop(0, (SECTIONS - 1) * GROUPS)(section_group)

    def last_group(g):
        parity = (SECTIONS - 1) % 2
        finish(main, (g,), (parity, g))
        got = in_tiles_of(in_tiles, (parity, g))

        def body(c, carry):
            ch = g * per + c
            store(out_ref, ch, advance(ch, c, g, parity, got, jnp.float32(time_step)))
            return carry

        lax.fori_loop(0, per, body, 0, unroll=UNROLL)

    pl.loop(0, GROUPS)(last_group)


def on_device(
    counts, initial_state, forcing, jacobian, metric, viscosity, element_turns
):
    np0, np1, chan, rows, cols = initial_state.shape
    per = chan // GROUPS
    f32 = jnp.float32
    field = pltpu.VMEM((NP, NP, chan, rows, cols), f32)
    vmem = pl.BlockSpec(memory_space=pltpu.VMEM)

    def buffers(out_lead, in_lead, tiles_per_rows):
        dma = pltpu.SemaphoreType.DMA
        return [
            pltpu.VMEM((2,) + out_lead + (tiles_per_rows, rows, cols), f32),
            pltpu.VMEM((6,) + out_lead + (rows, cols), f32),
            pltpu.VMEM((2,) + in_lead + (tiles_per_rows, rows, cols), f32),
            pltpu.VMEM((6,) + in_lead + (rows, cols), f32),
            dma((8,) + out_lead),
            dma((8,) + in_lead),
        ]

    return pl.pallas_call(
        functools.partial(kernel, (chan, rows, cols) + counts),
        out_shape=jax.ShapeDtypeStruct(initial_state.shape, f32),
        in_specs=[vmem] * 5 + [pl.BlockSpec(memory_space=pltpu.SMEM)],
        out_specs=vmem,
        scratch_shapes=[
            field,
            field,
            field,
            pltpu.VMEM((16, rows, cols), f32),
            pltpu.VMEM((48, rows, cols), f32),
            pltpu.VMEM((48, rows, cols), f32),
            pltpu.VMEM((16, rows, cols), f32),
            pltpu.VMEM((16, rows, cols), f32),
        ]
        + buffers((GROUPS,), (2, GROUPS), per)
        + buffers((GROUPS,), (GROUPS,), per)
        + buffers((), (), 2),
        compiler_params=pltpu.CompilerParams(
            collective_id=0, has_side_effects=True, vmem_limit_bytes=48 * 2**20
        ),
    )(initial_state, forcing, jacobian, metric, element_turns, viscosity)


def solution(mesh):
    placed = (
        P(None, None, None, "gy", "gx"),
        P(None, None, None, "gy", "gx"),
        P(None, None, "gy", "gx"),
        P(None, None, "gy", "gx"),
        P(),
        P("gy", "gx"),
    )
    return jax.shard_map(
        functools.partial(on_device, (mesh.shape["gx"], mesh.shape["gy"])),
        mesh=mesh,
        in_specs=placed,
        out_specs=P(None, None, None, "gy", "gx"),
        check_vma=False,
    )
```

```python
import functools
import math

import jax
import jax.numpy as jnp
import numpy as np
from jax import lax
from jax.experimental import pallas as pl
from jax.experimental.pallas import tpu as pltpu
from jax.sharding import PartitionSpec as P

NP = 4
SECTIONS = 5
GROUPS = 4
UNROLL = 8
time_step = 1.0
PAIRS = ((0, 1), (0, 2), (0, 3), (1, 2), (1, 3), (2, 3))
NORTH, SOUTH, EAST, WEST, NE, SW, NW, SE = range(8)
STEP = ((0, 1), (0, -1), (1, 0), (-1, 0), (1, 1), (-1, -1), (-1, 1), (1, -1))
MESH = pl.DeviceIdType.MESH
RIGHT = (EAST, NE, SE)


def lagrange_tables():
    root_five = 1.0 / math.sqrt(5.0)
    points = np.array([-1.0, -root_five, root_five, 1.0])
    weights = np.array([1.0 / 6.0, 5.0 / 6.0, 5.0 / 6.0, 1.0 / 6.0])
    number = points.shape[0]
    products = np.ones(number)
    for row in range(number):
        for other in range(number):
            if other != row:
                products[row] = products[row] * (points[row] - points[other])
    derivative = np.zeros((number, number))
    for row in range(number):
        for column in range(number):
            if row == column:
                derivative[row, column] = sum(
                    1.0 / (points[row] - points[other])
                    for other in range(number)
                    if other != row
                )
            else:
                derivative[row, column] = products[row] / (
                    products[column] * (points[row] - points[column])
                )
    return (derivative, weights)


def turned(v):
    return [[v[i][NP - 1 - j] for i in range(NP)] for j in range(NP)]


def face_frame(v, masks):
    result = v
    for mask in masks:
        v = turned(v)
        result = [
            [jnp.where(mask, v[j][i], result[j][i]) for i in range(NP)]
            for j in range(NP)
        ]
    return result


def kernel(
    sizes,
    state_hbm,
    forcing_hbm,
    jacobian_hbm,
    metric_hbm,
    turns_hbm,
    viscosity_hbm,
    out_ref,
    state_ref,
    forcing_ref,
    jacobian_ref,
    metric_ref,
    turns_ref,
    viscosity_ref,
    field_sem,
    small_sem,
    part_ref,
    base_ref,
    tend_ref,
    inverse_ref,
    own_k_ref,
    both_k_ref,
    diagonal_ref,
    mass_ref,
    out_rows,
    out_tiles,
    in_rows,
    in_tiles,
    send_sem,
    recv_sem,
    set_out_rows,
    set_out_tiles,
    set_in_rows,
    set_in_tiles,
    set_send,
    set_recv,
    ini_out_rows,
    ini_out_tiles,
    ini_in_rows,
    ini_in_tiles,
    ini_send,
    ini_recv,
):
    chan, rows, cols, count_x, count_y = sizes
    per = chan // GROUPS
    last_row, last_col = rows - 1, cols - 1
    derivative, weights = lagrange_tables()
    cx = lax.axis_index("gx")
    cy = lax.axis_index("gy")
    lane = lax.broadcasted_iota(jnp.int32, (rows, cols), 1)
    sub = lax.broadcasted_iota(jnp.int32, (rows, cols), 0)
    at_west, at_east = lane == 0, lane == last_col
    at_south, at_north = sub == 0, sub == last_row
    zero = jnp.zeros((rows, cols), jnp.float32)
    there_north = cy < count_y - 1
    there_south = cy > 0

    def device(d):
        dx, dy = STEP[d]
        return (lax.rem(cx + dx + count_x, count_x), cy + dy)

    def for_each(todo):
        for d in (EAST, WEST):
            todo(d)

        @pl.when(there_north)
        def _():
            for d in (NORTH, NE, NW):
                todo(d)

        @pl.when(there_south)
        def _():
            for d in (SOUTH, SE, SW):
                todo(d)

    def copy(bufs, where_out, where_in, d, arriving=False):
        o_rows, o_tiles, i_rows, i_tiles, ssem, rsem, shared = bufs
        slot = d if arriving else d ^ 1
        if d in (NORTH, SOUTH):
            src, dst = o_rows.at[(d,) + where_out], i_rows.at[(slot,) + where_in]
        else:
            src = o_tiles.at[(d - 2 if shared is None else int(d not in RIGHT),) + where_out]
            dst = i_tiles.at[(slot - 2,) + where_in]
        return pltpu.make_async_remote_copy(
            src_ref=src,
            dst_ref=dst,
            send_sem=ssem.at[(d,) + where_out],
            recv_sem=rsem.at[(slot,) + where_in],
            device_id=device(d),
            device_id_type=MESH,
        )

    def start(bufs, where_out, where_in):
        for_each(lambda d: copy(bufs, where_out, where_in, d).start())

    def finish(bufs, where_out, where_in):
        def todo(d):
            c = copy(bufs, where_out, where_in, d, arriving=True)
            c.wait_recv()
            c.wait_send()

        for_each(todo)

    main = (out_rows, out_tiles, in_rows, in_tiles, send_sem, recv_sem, True)
    sets = (set_out_rows, set_out_tiles, set_in_rows, set_in_tiles, set_send, set_recv, True)
    ini = (ini_out_rows, ini_out_tiles, ini_in_rows, ini_in_tiles, ini_send, ini_recv, None)

    def join_x(a, b):
        return (
            a + jnp.where(at_west, 0.0, pltpu.roll(b, 1, 1)),
            b + jnp.where(at_east, 0.0, pltpu.roll(a, cols - 1, 1)),
        )

    def join_y(a, b):
        return (
            a + jnp.where(at_south, 0.0, pltpu.roll(b, 1, 0)),
            b + jnp.where(at_north, 0.0, pltpu.roll(a, rows - 1, 0)),
        )

    def join(s):
        s = [list(r) for r in s]
        for j in range(NP):
            s[j][0], s[j][3] = join_x(s[j][0], s[j][3])
        for i in range(NP):
            s[0][i], s[3][i] = join_y(s[0][i], s[3][i])
        return s

    def line(v, k):
        p = [k[n] * (v[b] - v[a]) for n, (a, b) in enumerate(PAIRS)]
        return (
            p[0] + p[1] + p[2],
            p[3] + p[4] - p[0],
            p[5] - p[1] - p[3],
            -(p[2] + p[4] + p[5]),
        )

    def stiff(v, k_ref):
        s = [[None] * NP for _ in range(NP)]
        for j in range(NP):
            got = line(v[j], [k_ref[j * 6 + n] for n in range(6)])
            for i in range(NP):
                s[j][i] = got[i]
        for i in range(NP):
            got = line(
                [v[j][i] for j in range(NP)],
                [k_ref[24 + i * 6 + n] for n in range(6)],
            )
            for j in range(NP):
                s[j][i] = s[j][i] + got[j]
        return join(s)

    def from_inside(w):
        rx = [[None] * NP for _ in range(NP)]
        ry = [[None] * NP for _ in range(NP)]
        for j in range(NP):
            k = [both_k_ref[j * 6 + n] for n in range(6)]
            rx[j][0] = k[0] * w[j][1] + k[1] * w[j][2] + k[2] * w[j][3]
            rx[j][3] = k[2] * w[j][0] + k[4] * w[j][1] + k[5] * w[j][2]
        for i in range(NP):
            k = [both_k_ref[24 + i * 6 + n] for n in range(6)]
            ry[0][i] = k[0] * w[1][i] + k[1] * w[2][i] + k[2] * w[3][i]
            ry[3][i] = k[2] * w[0][i] + k[4] * w[1][i] + k[5] * w[2][i]
        return joined_edges(rx, ry)

    def joined_edges(rx, ry):
        for i in (0, 3):
            rx[0][i], rx[3][i] = join_y(rx[0][i], rx[3][i])
        for j in (0, 3):
            ry[j][0], ry[j][3] = join_x(ry[j][0], ry[j][3])
        return rx, ry

    def load(ref, c):
        return [[ref[j, i, c] for i in range(NP)] for j in range(NP)]

    def store(ref, c, v):
        for j in range(NP):
            for i in range(NP):
                ref[j, i, c] = v[j][i]

    def times(v, ref):
        return [[v[j][i] * ref[j * NP + i] for i in range(NP)] for j in range(NP)]

    def lay_rows(ref, where, k, top, bottom):
        ref[(NORTH,) + where + (slice(k, k + 1), slice(None))] = top[last_row:, :]
        ref[(SOUTH,) + where + (slice(k, k + 1), slice(None))] = bottom[0:1, :]

    def lay_lane(tiles, n, right, left, corner):
        here = lane == n
        from_right = lax.rem(n + 1, cols)

        def put(d, v, shift):
            tiles[d - 2] = jnp.where(here, pltpu.roll(v, shift, 1), tiles[d - 2])

        if right is not None:
            put(EAST, right, from_right)
            put(WEST, left, n)
        if corner is not None:
            put(NE, corner[0], from_right)
            put(SW, corner[1], n)
            put(NW, corner[2], n)
            put(SE, corner[3], from_right)

    def emit(refs, where, c, tiles, fields):
        for q, (vx, vy, corner) in enumerate(fields):
            for i in range(NP):
                lay_rows(refs[0], where + (c,), q * NP + i, vy[3][i], vy[0][i])
        sides = []
        for tile, i in zip(tiles, (3, 0)):
            (v, _, _), (x, _, corner) = fields
            top, bottom = (corner[0], corner[3]) if i == 3 else (corner[2], corner[1])
            ends = jnp.where(
                sub == last_row,
                v[3][i],
                jnp.where(
                    sub == last_row - 1,
                    pltpu.roll(x[3][i], rows - 1, 0),
                    jnp.where(sub == last_row - 2, pltpu.roll(top, rows - 2, 0), bottom),
                ),
            )
            for m, value in enumerate([f[0][j][i] for f in fields for j in range(3)] + [ends]):
                n = m * per + c
                shift = lax.rem(n + 1, cols) if i == 3 else n
                tile = jnp.where(lane == n, pltpu.roll(value, shift, 1), tile)
            sides.append(tile)
        return tuple(sides)

    def corners_of(v):
        return (v[3][3], v[0][0], v[3][0], v[0][3])

    def row(ref, where, k):
        return jnp.broadcast_to(
            ref[where + (slice(k, k + 1), slice(None))], (rows, cols)
        )

    def ini_tiles():
        got = [ini_in_tiles[d - 2] for d in range(2, 8)]
        for d in (NE, NW):
            got[d - 2] = pltpu.roll(got[d - 2], rows - 1, 0)
        for d in (SE, SW):
            got[d - 2] = pltpu.roll(got[d - 2], 1, 0)
        return got

    def in_sides(ref, where):
        sides = []
        for side, above, below in ((EAST, NE, SE), (WEST, NW, SW)):
            here, up, down = [ref[(d - 2,) + where] for d in (side, above, below)]
            first = pltpu.roll(pltpu.roll(up, 6 * per, 1), rows - 1, 0)
            ends = jnp.where(
                sub == last_row,
                here + first,
                jnp.where(
                    sub == last_row - 1,
                    here + pltpu.roll(up, rows - 2, 0),
                    jnp.where(sub == 0, pltpu.roll(down, 1, 0), pltpu.roll(down, 4, 0)),
                ),
            )
            sides.append(jnp.where(lane < 6 * per, here, ends))
        return sides

    def add_in(v, ref, where, c, got, q):
        v = [list(r) for r in v]
        for i in range(NP):
            k = q * NP + i
            v[3][i] = v[3][i] + jnp.where(at_north, row(ref, (NORTH,) + where + (c,), k), 0.0)
            v[0][i] = v[0][i] + jnp.where(at_south, row(ref, (SOUTH,) + where + (c,), k), 0.0)
        for side, i, to, edge in ((0, 3, last_col, at_east), (1, 0, cols, at_west)):

            def lane_to(m):
                return pltpu.roll(got[side], lax.rem(to - (m * per + c), cols), 1)

            column = [lane_to(q * 3 + j) for j in range(3)]
            ends = lane_to(6)
            if q == 1:
                top, bottom = pltpu.roll(ends, 1, 0), pltpu.roll(ends, rows - 1, 0)
            else:
                top = bottom = ends
            for j in (1, 2):
                v[j][i] = v[j][i] + jnp.where(edge, column[j], 0.0)
            v[0][i] = v[0][i] + jnp.where(
                edge, jnp.where(at_south, column[0] + bottom, column[0]), 0.0
            )
            v[3][i] = v[3][i] + jnp.where(
                edge, jnp.where(at_north, top, pltpu.roll(column[0], rows - 1, 0)), 0.0
            )
        return v

    def keep_tiles(ref, where, tiles):
        for side in range(2):
            ref[(side,) + where] = tiles[side]

    small = [
        pltpu.make_async_copy(a, b, small_sem.at[n])
        for n, (a, b) in enumerate(
            (
                (jacobian_hbm, jacobian_ref),
                (metric_hbm, metric_ref),
                (turns_hbm, turns_ref),
                (viscosity_hbm, viscosity_ref),
            )
        )
    ]
    for c in small:
        c.start()

    def fields(g):
        part = (slice(None), slice(None), pl.ds(g * per, per))
        return [
            pltpu.make_async_copy(a.at[part], b.at[part], field_sem.at[n, g])
            for n, (a, b) in enumerate(
                ((state_hbm, state_ref), (forcing_hbm, forcing_ref))
            )
        ]

    for g in range(GROUPS):
        for c in fields(g):
            c.start()

    in_rows[...] = jnp.zeros_like(in_rows)
    in_tiles[...] = jnp.zeros_like(in_tiles)
    set_in_rows[...] = jnp.zeros_like(set_in_rows)
    set_in_tiles[...] = jnp.zeros_like(set_in_tiles)
    ini_in_rows[...] = jnp.zeros_like(ini_in_rows)
    ini_in_tiles[...] = jnp.zeros_like(ini_in_tiles)
    barrier = pltpu.get_barrier_semaphore()
    for_each(
        lambda d: pl.semaphore_signal(
            barrier, inc=1, device_id=device(d), device_id_type=MESH
        )
    )
    for c in small:
        c.wait()

    turns = turns_ref[...]
    masks = [turns == quarter for quarter in range(1, 4)]
    jacobian = face_frame(
        [[jacobian_ref[j, i] for i in range(NP)] for j in range(NP)], masks
    )
    metric = face_frame(
        [[metric_ref[j, i] for i in range(NP)] for j in range(NP)], masks
    )
    mass = [
        [float(weights[j] * weights[i]) * jacobian[j][i] for i in range(NP)]
        for j in range(NP)
    ]
    flux = [
        [float(weights[j] * weights[i]) * metric[j][i] for i in range(NP)]
        for j in range(NP)
    ]
    for j in range(NP):
        for i in range(NP):
            mass_ref[j * NP + i] = mass[j][i]

    def coefficients(f):
        return [
            sum(float(-derivative[n, a] * derivative[n, b]) * f[n] for n in range(NP))
            for a, b in PAIRS
        ]

    kx = [coefficients(flux[j]) for j in range(NP)]
    ky = [coefficients([flux[j][i] for j in range(NP)]) for i in range(NP)]
    for m in range(NP):
        for n in range(6):
            own_k_ref[m * 6 + n] = kx[m][n]
            own_k_ref[24 + m * 6 + n] = ky[m][n]
    first = lambda k: k[0] + k[1] + k[2]
    final = lambda k: k[2] + k[4] + k[5]
    dx = [[first(kx[j]), None, None, final(kx[j])] for j in range(NP)]
    dy = [[None] * NP for _ in range(NP)]
    for i in range(NP):
        dy[0][i], dy[3][i] = first(ky[i]), final(ky[i])
    dx, dy = joined_edges(dx, dy)
    local = join(mass)
    tiles = [zero] * 6
    for n in range(NP):
        lay_rows(ini_out_rows, (0,), n, local[3][n], local[0][n])
        lay_rows(ini_out_rows, (0,), 4 + n, dy[3][n], dy[0][n])
        lay_lane(tiles, n, local[n][3], local[n][0], None)
        lay_lane(tiles, 4 + n, dx[n][3], dx[n][0], None)
    for n in range(6):
        lay_rows(ini_out_rows, (1,), n, kx[3][n], kx[0][n])
        lay_lane(tiles, 8 + n, ky[3][n], ky[0][n], None)
    lay_lane(tiles, 0, None, None, corners_of(local))
    both = [[None] * NP for _ in range(NP)]
    for j in (0, 3):
        for i in (0, 3):
            both[j][i] = dx[j][i] + dy[j][i]
    lay_lane(tiles, 1, None, None, corners_of(both))
    for n in (6, 7):
        lay_rows(ini_out_rows, (1,), n, zero, zero)
    for d in range(2, 8):
        ini_out_tiles[d - 2] = tiles[d - 2]
    peers = 2 + 3 * there_north.astype(jnp.int32) + 3 * there_south.astype(jnp.int32)
    pl.semaphore_wait(barrier, peers)
    start(ini, (), ())

    def enter_group(g):
        for c in fields(g):
            c.wait()

        def enter(c, tiles):
            ch = g * per + c
            state = face_frame(load(state_ref, ch), masks)
            forcing = face_frame(load(forcing_ref, ch), masks)
            base = join(times(state, mass_ref))
            tend = join(times(forcing, mass_ref))
            store(base_ref, ch, base)
            store(tend_ref, ch, tend)
            tiles = emit(
                sets,
                (g,),
                c,
                tiles,
                ((base, base, corners_of(base)), (tend, tend, corners_of(tend))),
            )
            store(part_ref, ch, stiff(state, own_k_ref))
            return tiles

        tiles = lax.fori_loop(0, per, enter, (zero,) * 2, unroll=UNROLL)
        keep_tiles(set_out_tiles, (g,), tiles)
        start(sets, (g,), (g,))

    pl.loop(0, GROUPS)(enter_group)

    finish(ini, (), ())
    got = ini_tiles()

    def lane_of(d, n):
        to = last_col if d in (EAST, NE, SE) else 0
        return pltpu.roll(got[d - 2], (to - n) % cols, 1)

    def north(block, k):
        return jnp.where(at_north, row(ini_in_rows, (NORTH, block), k), 0.0)

    def south(block, k):
        return jnp.where(at_south, row(ini_in_rows, (SOUTH, block), k), 0.0)

    def east(n):
        return jnp.where(at_east, lane_of(EAST, n), 0.0)

    def west(n):
        return jnp.where(at_west, lane_of(WEST, n), 0.0)

    def with_neighbours(v, first_k, corner_n):
        v = [list(r) for r in v]
        for i in range(NP):
            v[3][i] = v[3][i] + north(0, first_k + i)
            v[0][i] = v[0][i] + south(0, first_k + i)
        for j in range(NP):
            v[j][3] = v[j][3] + east(first_k + j)
            v[j][0] = v[j][0] + west(first_k + j)
        for d, j, i, m in (
            (NE, 3, 3, at_north & at_east),
            (SW, 0, 0, at_south & at_west),
            (NW, 3, 0, at_north & at_west),
            (SE, 0, 3, at_south & at_east),
        ):
            v[j][i] = v[j][i] + jnp.where(m, lane_of(d, corner_n), 0.0)
        return v

    assembled = with_neighbours(local, 0, 0)
    diagonal = with_neighbours([[zero] * NP for _ in range(NP)], 4, 1)
    for j in range(NP):
        for i in range(NP):
            inverse_ref[j * NP + i] = 1.0 / assembled[j][i]
            diagonal_ref[j * NP + i] = diagonal[j][i]
    for m in range(NP):
        for n in range(6):
            x, y = kx[m][n], ky[m][n]
            if m == 0:
                x, y = x + south(1, n), y + west(8 + n)
            if m == 3:
                x, y = x + north(1, n), y + east(8 + n)
            both_k_ref[m * 6 + n] = x
            both_k_ref[24 + m * 6 + n] = y

    def emit_main(g, c, tiles, s):
        rx, ry = from_inside(times(s, inverse_ref))
        corner = tuple(
            rx[j][i] + ry[j][i] for j, i in ((3, 3), (0, 0), (3, 0), (0, 3))
        )
        return emit(main, (g,), c, tiles, ((s, s, corners_of(s)), (rx, ry, corner)))

    def send_group(g):
        def send(c, tiles):
            return emit_main(g, c, tiles, load(part_ref, g * per + c))

        tiles = lax.fori_loop(0, per, send, (zero,) * 2, unroll=UNROLL)
        keep_tiles(out_tiles, (g,), tiles)
        start(main, (g,), (0, g))

    pl.loop(0, GROUPS)(send_group)

    def settle_group(g):
        finish(sets, (g,), (g,))
        got = in_sides(set_in_tiles, (g,))

        def settle(c, carry):
            ch = g * per + c
            for q, ref in enumerate((base_ref, tend_ref)):
                v = add_in(load(ref, ch), set_in_rows, (g,), c, got, q)
                store(ref, ch, times(v, inverse_ref))
            return carry

        lax.fori_loop(0, per, settle, 0, unroll=UNROLL)

    pl.loop(0, GROUPS)(settle_group)

    def advance(ch, c, g, parity, got, factor):
        where = (parity, g)
        s = add_in(load(part_ref, ch), in_rows, where, c, got, 0)
        w = times(s, inverse_ref)
        t = add_in(stiff(w, both_k_ref), in_rows, where, c, got, 1)
        scale = factor * viscosity_ref[ch]
        for j in range(NP):
            for i in range(NP):
                if j in (0, 3) or i in (0, 3):
                    t[j][i] = t[j][i] - diagonal_ref[j * NP + i] * w[j][i]
        return [
            [
                base_ref[j, i, ch]
                + (
                    factor * tend_ref[j, i, ch]
                    - scale * (t[j][i] * inverse_ref[j * NP + i])
                )
                for i in range(NP)
            ]
            for j in range(NP)
        ]

    def section_group(step):
        section, g = step // GROUPS, lax.rem(step, GROUPS)
        parity = lax.rem(section, 2)
        factor = jnp.float32(time_step / SECTIONS)
        for m in range(1, SECTIONS - 1):
            factor = jnp.where(
                section == m, jnp.float32(time_step / (SECTIONS - m)), factor
            )
        finish(main, (g,), (parity, g))
        got = in_sides(in_tiles, (parity, g))

        def body(c, tiles):
            ch = g * per + c
            u = advance(ch, c, g, parity, got, factor)
            s = stiff(u, own_k_ref)
            store(part_ref, ch, s)
            return emit_main(g, c, tiles, s)

        tiles = lax.fori_loop(0, per, body, (zero,) * 2, unroll=UNROLL)
        keep_tiles(out_tiles, (g,), tiles)
        start(main, (g,), (1 - parity, g))

    pl.loop(0, (SECTIONS - 1) * GROUPS)(section_group)

    def last_group(g):
        parity = (SECTIONS - 1) % 2
        finish(main, (g,), (parity, g))
        got = in_sides(in_tiles, (parity, g))

        def body(c, carry):
            ch = g * per + c
            store(out_ref, ch, advance(ch, c, g, parity, got, jnp.float32(time_step)))
            return carry

        lax.fori_loop(0, per, body, 0, unroll=UNROLL)

    pl.loop(0, GROUPS)(last_group)


def on_device(
    counts, initial_state, forcing, jacobian, metric, viscosity, element_turns
):
    np0, np1, chan, rows, cols = initial_state.shape
    per = chan // GROUPS
    f32 = jnp.float32
    field = pltpu.VMEM((NP, NP, chan, rows, cols), f32)
    vmem = pl.BlockSpec(memory_space=pltpu.VMEM)

    def buffers(out_lead, in_lead, tiles_per_rows, out_tiles):
        dma = pltpu.SemaphoreType.DMA
        return [
            pltpu.VMEM((2,) + out_lead + (tiles_per_rows, rows, cols), f32),
            pltpu.VMEM((out_tiles,) + out_lead + (rows, cols), f32),
            pltpu.VMEM((2,) + in_lead + (tiles_per_rows, rows, cols), f32),
            pltpu.VMEM((6,) + in_lead + (rows, cols), f32),
            dma((8,) + out_lead),
            dma((8,) + in_lead),
        ]

    return pl.pallas_call(
        functools.partial(kernel, (chan, rows, cols) + counts),
        out_shape=jax.ShapeDtypeStruct(initial_state.shape, f32),
        in_specs=[pl.BlockSpec(memory_space=pl.ANY)] * 6,
        out_specs=vmem,
        scratch_shapes=[
            field,
            field,
            pltpu.VMEM(jacobian.shape, f32),
            pltpu.VMEM(metric.shape, f32),
            pltpu.VMEM(element_turns.shape, jnp.int32),
            pltpu.SMEM(viscosity.shape, f32),
            pltpu.SemaphoreType.DMA((2, GROUPS)),
            pltpu.SemaphoreType.DMA((4,)),
            field,
            field,
            field,
            pltpu.VMEM((16, rows, cols), f32),
            pltpu.VMEM((48, rows, cols), f32),
            pltpu.VMEM((48, rows, cols), f32),
            pltpu.VMEM((16, rows, cols), f32),
            pltpu.VMEM((16, rows, cols), f32),
        ]
        + buffers((GROUPS,), (2, GROUPS), per, 2)
        + buffers((GROUPS,), (GROUPS,), per, 2)
        + buffers((), (), 2, 6),
        compiler_params=pltpu.CompilerParams(
            collective_id=0, has_side_effects=True, vmem_limit_bytes=56 * 2**20
        ),
    )(initial_state, forcing, jacobian, metric, element_turns, viscosity)


def solution(mesh):
    placed = (
        P(None, None, None, "gy", "gx"),
        P(None, None, None, "gy", "gx"),
        P(None, None, "gy", "gx"),
        P(None, None, "gy", "gx"),
        P(),
        P("gy", "gx"),
    )
    return jax.shard_map(
        functools.partial(on_device, (mesh.shape["gx"], mesh.shape["gy"])),
        mesh=mesh,
        in_specs=placed,
        out_specs=P(None, None, None, "gy", "gx"),
        check_vma=False,
    )
```

```python
import functools
import math

import jax
import jax.numpy as jnp
import numpy as np
from jax import lax
from jax.experimental import pallas as pl
from jax.experimental.pallas import tpu as pltpu
from jax.sharding import PartitionSpec as P

NP = 4
SECTIONS = 5
GROUPS = 4
UNROLL = 8
time_step = 1.0
PAIRS = ((0, 1), (0, 2), (0, 3), (1, 2), (1, 3), (2, 3))
NORTH, SOUTH, EAST, WEST, NE, SW, NW, SE = range(8)
STEP = ((0, 1), (0, -1), (1, 0), (-1, 0), (1, 1), (-1, -1), (-1, 1), (1, -1))
MESH = pl.DeviceIdType.MESH
RIGHT = (EAST, NE, SE)
TILES_N, TILES_S = 8, 9


def lagrange_tables():
    root_five = 1.0 / math.sqrt(5.0)
    points = np.array([-1.0, -root_five, root_five, 1.0])
    weights = np.array([1.0 / 6.0, 5.0 / 6.0, 5.0 / 6.0, 1.0 / 6.0])
    number = points.shape[0]
    products = np.ones(number)
    for row in range(number):
        for other in range(number):
            if other != row:
                products[row] = products[row] * (points[row] - points[other])
    derivative = np.zeros((number, number))
    for row in range(number):
        for column in range(number):
            if row == column:
                derivative[row, column] = sum(
                    1.0 / (points[row] - points[other])
                    for other in range(number)
                    if other != row
                )
            else:
                derivative[row, column] = products[row] / (
                    products[column] * (points[row] - points[column])
                )
    return (derivative, weights)


def turned(v):
    return [[v[i][NP - 1 - j] for i in range(NP)] for j in range(NP)]


def face_frame(v, masks):
    result = v
    for mask in masks:
        v = turned(v)
        result = [
            [jnp.where(mask, v[j][i], result[j][i]) for i in range(NP)]
            for j in range(NP)
        ]
    return result


def kernel(
    sizes,
    state_hbm,
    forcing_hbm,
    jacobian_hbm,
    metric_hbm,
    turns_hbm,
    viscosity_hbm,
    out_ref,
    state_ref,
    forcing_ref,
    jacobian_ref,
    metric_ref,
    turns_ref,
    viscosity_ref,
    field_sem,
    small_sem,
    part_ref,
    base_ref,
    tend_ref,
    inverse_ref,
    own_k_ref,
    both_k_ref,
    diagonal_ref,
    mass_ref,
    weight_ref,
    out_rows,
    out_tiles,
    in_rows,
    in_tiles,
    in_more,
    send_sem,
    recv_sem,
    set_out_rows,
    set_out_tiles,
    set_in_rows,
    set_in_tiles,
    set_send,
    set_recv,
    ini_out_rows,
    ini_out_tiles,
    ini_in_rows,
    ini_in_tiles,
    ini_in_more,
    ini_send,
    ini_recv,
):
    chan, rows, cols, count_x, count_y = sizes
    per = chan // GROUPS
    last_row, last_col = rows - 1, cols - 1
    derivative, weights = lagrange_tables()
    cx = lax.axis_index("gx")
    cy = lax.axis_index("gy")
    lane = lax.broadcasted_iota(jnp.int32, (rows, cols), 1)
    sub = lax.broadcasted_iota(jnp.int32, (rows, cols), 0)
    at_west, at_east = lane == 0, lane == last_col
    at_south, at_north = sub == 0, sub == last_row
    zero = jnp.zeros((rows, cols), jnp.float32)
    there_north = cy < count_y - 1
    there_south = cy > 0

    def device(d):
        dx, dy = STEP[d % 8]
        return (lax.rem(cx + dx + count_x, count_x), cy + dy)

    def for_each(todo, tiles_too=False):
        @pl.when(there_north)
        def _():
            for d in (NE, NW, NORTH) + (TILES_N,) * tiles_too:
                todo(d)

        @pl.when(there_south)
        def _():
            for d in (SE, SW, SOUTH) + (TILES_S,) * tiles_too:
                todo(d)

        for d in (EAST, WEST):
            todo(d)

    def copy(bufs, where_out, where_in, d, arriving=False):
        o_rows, o_tiles, i_rows, i_tiles, i_more, ssem, rsem = bufs
        slot = d if arriving else d ^ 1
        send, recv = ssem.at[(d,) + where_out], rsem.at[(slot,) + where_in]
        if d in (NORTH, SOUTH):
            src, dst = o_rows.at[(d,) + where_out], i_rows.at[(slot,) + where_in]
        elif d in (TILES_N, TILES_S):
            src = o_tiles.at[(slice(None),) + where_out]
            dst = i_more.at[(slot - 8, slice(None)) + where_out]
            recv = rsem.at[(slot,) + where_in]
        else:
            src = o_tiles.at[(int(d not in RIGHT),) + where_out]
            dst = i_tiles.at[(slot - 2,) + where_in]
        return pltpu.make_async_remote_copy(
            src_ref=src,
            dst_ref=dst,
            send_sem=send,
            recv_sem=recv,
            device_id=device(d),
            device_id_type=MESH,
        )

    def start(bufs, where_out, where_in, tiles_too=False):
        for_each(lambda d: copy(bufs, where_out, where_in, d).start(), tiles_too)

    def finish(bufs, where_out, where_in, tiles_too=False):
        def todo(d):
            c = copy(bufs, where_out, where_in, d, arriving=True)
            c.wait_recv()
            c.wait_send()

        for_each(todo, tiles_too)

    def finish_more(g):
        def todo(d):
            if d in (TILES_N, TILES_S):
                c = copy(main, (g,), (0, g), d, arriving=True)
                c.wait_recv()
                c.wait_send()

        for_each(todo, True)

    main = (out_rows, out_tiles, in_rows, in_tiles, in_more, send_sem, recv_sem)
    sets = (
        set_out_rows, set_out_tiles, set_in_rows, set_in_tiles, None, set_send, set_recv
    )
    ini = (
        ini_out_rows, ini_out_tiles, ini_in_rows, ini_in_tiles, ini_in_more,
        ini_send, ini_recv,
    )

    def join_x(a, b):
        return (
            a + jnp.where(at_west, 0.0, pltpu.roll(b, 1, 1)),
            b + jnp.where(at_east, 0.0, pltpu.roll(a, cols - 1, 1)),
        )

    def join_y(a, b):
        return (
            a + jnp.where(at_south, 0.0, pltpu.roll(b, 1, 0)),
            b + jnp.where(at_north, 0.0, pltpu.roll(a, rows - 1, 0)),
        )

    def join(s):
        s = [list(r) for r in s]
        for j in range(NP):
            s[j][0], s[j][3] = join_x(s[j][0], s[j][3])
        for i in range(NP):
            s[0][i], s[3][i] = join_y(s[0][i], s[3][i])
        return s

    def line(v, k):
        p = [k[n] * (v[b] - v[a]) for n, (a, b) in enumerate(PAIRS)]
        return (
            p[0] + p[1] + p[2],
            p[3] + p[4] - p[0],
            p[5] - p[1] - p[3],
            -(p[2] + p[4] + p[5]),
        )

    def stiff(v, k_ref):
        s = [[None] * NP for _ in range(NP)]
        for j in range(NP):
            got = line(v[j], [k_ref[j * 6 + n] for n in range(6)])
            for i in range(NP):
                s[j][i] = got[i]
        for i in range(NP):
            got = line(
                [v[j][i] for j in range(NP)],
                [k_ref[24 + i * 6 + n] for n in range(6)],
            )
            for j in range(NP):
                s[j][i] = s[j][i] + got[j]
        return join(s)

    def from_inside(w, k_ref):
        rx = [[None] * NP for _ in range(NP)]
        ry = [[None] * NP for _ in range(NP)]
        for j in range(NP):
            k = [k_ref[j * 6 + n] for n in range(6)]
            rx[j][0] = k[0] * w[j][1] + k[1] * w[j][2] + k[2] * w[j][3]
            rx[j][3] = k[2] * w[j][0] + k[4] * w[j][1] + k[5] * w[j][2]
        for i in range(NP):
            k = [k_ref[24 + i * 6 + n] for n in range(6)]
            ry[0][i] = k[0] * w[1][i] + k[1] * w[2][i] + k[2] * w[3][i]
            ry[3][i] = k[2] * w[0][i] + k[4] * w[1][i] + k[5] * w[2][i]
        return joined_edges(rx, ry)

    def joined_edges(rx, ry):
        for i in (0, 3):
            rx[0][i], rx[3][i] = join_y(rx[0][i], rx[3][i])
        for j in (0, 3):
            ry[j][0], ry[j][3] = join_x(ry[j][0], ry[j][3])
        return rx, ry

    def load(ref, c):
        return [[ref[j, i, c] for i in range(NP)] for j in range(NP)]

    def store(ref, c, v):
        for j in range(NP):
            for i in range(NP):
                ref[j, i, c] = v[j][i]

    def times(v, ref):
        return [[v[j][i] * ref[j * NP + i] for i in range(NP)] for j in range(NP)]

    def lay_rows(ref, where, k, top, bottom):
        ref[(NORTH,) + where + (slice(k, k + 1), slice(None))] = top[last_row:, :]
        ref[(SOUTH,) + where + (slice(k, k + 1), slice(None))] = bottom[0:1, :]

    def lay_lane(tiles, n, right, left, corner):
        here = lane == n
        from_right = lax.rem(n + 1, cols)

        def put(d, v, shift):
            tiles[d - 2] = jnp.where(here, pltpu.roll(v, shift, 1), tiles[d - 2])

        if right is not None:
            put(EAST, right, from_right)
            put(WEST, left, n)
        if corner is not None:
            put(NE, corner[0], from_right)
            put(SW, corner[1], n)
            put(NW, corner[2], n)
            put(SE, corner[3], from_right)

    def stacked(top, bottom):
        kept = top[0]
        for n in (1, 2):
            kept = jnp.where(sub == last_row - n, pltpu.roll(top[n], rows - n, 0), kept)
        for n in range(3):
            kept = jnp.where(sub == 2 - n, pltpu.roll(bottom[n], 2 - n, 0), kept)
        return kept

    def along_x(v, i):
        order = (2, 1, 0) if i == 3 else (1, 2, 3)
        return stacked([v[3][n] for n in order], [v[0][n] for n in order])

    def along_y(v, i):
        return stacked([v[n][i] for n in (2, 1, 0)], [v[n][i] for n in (1, 2, 3)])

    def emit(refs, where, c, tiles, fields, segments=False):
        for q, (vx, vy, corner) in enumerate(fields):
            for i in range(NP):
                lay_rows(refs[0], where + (c,), q * NP + i, vy[3][i], vy[0][i])
        sides = []
        for tile, i in zip(tiles, (3, 0)):
            (v, _, _), (x, _, corner) = fields
            top, bottom = (corner[0], corner[3]) if i == 3 else (corner[2], corner[1])
            ends = jnp.where(
                sub == last_row,
                v[3][i],
                jnp.where(
                    sub == last_row - 1,
                    pltpu.roll(x[3][i], rows - 1, 0),
                    jnp.where(sub == last_row - 2, pltpu.roll(top, rows - 2, 0), bottom),
                ),
            )
            columns = [f[0][j][i] for f in fields for j in range(3)] + [ends]
            if segments:
                columns += [along_x(v, i), along_y(v, i)]
            for m, value in enumerate(columns):
                n = m * per + c
                shift = lax.rem(n + 1, cols) if i == 3 else n
                tile = jnp.where(lane == n, pltpu.roll(value, shift, 1), tile)
            sides.append(tile)
        return tuple(sides)

    def corners_of(v):
        return (v[3][3], v[0][0], v[3][0], v[0][3])

    def row(ref, where, k):
        return jnp.broadcast_to(
            ref[where + (slice(k, k + 1), slice(None))], (rows, cols)
        )

    def in_sides(ref, where):
        sides = []
        for side, above, below in ((EAST, NE, SE), (WEST, NW, SW)):
            here, up, down = [ref[(d - 2,) + where] for d in (side, above, below)]
            first = pltpu.roll(pltpu.roll(up, 6 * per, 1), rows - 1, 0)
            ends = jnp.where(
                sub == last_row,
                here + first,
                jnp.where(
                    sub == last_row - 1,
                    here + pltpu.roll(up, rows - 2, 0),
                    jnp.where(sub == 0, pltpu.roll(down, 1, 0), pltpu.roll(down, 4, 0)),
                ),
            )
            sides.append(jnp.where(lane < 6 * per, here, ends))
        return sides

    def add_in(v, ref, where, c, got, q):
        v = [list(r) for r in v]
        for i in range(NP):
            k = q * NP + i
            v[3][i] = v[3][i] + jnp.where(at_north, row(ref, (NORTH,) + where + (c,), k), 0.0)
            v[0][i] = v[0][i] + jnp.where(at_south, row(ref, (SOUTH,) + where + (c,), k), 0.0)
        for side, i, to, edge in ((0, 3, last_col, at_east), (1, 0, cols, at_west)):

            def lane_to(m):
                return pltpu.roll(got[side], lax.rem(to - (m * per + c), cols), 1)

            column = [lane_to(q * 3 + j) for j in range(3)]
            ends = lane_to(6)
            if q == 1:
                top, bottom = pltpu.roll(ends, 1, 0), pltpu.roll(ends, rows - 1, 0)
            else:
                top = bottom = ends
            for j in (1, 2):
                v[j][i] = v[j][i] + jnp.where(edge, column[j], 0.0)
            v[0][i] = v[0][i] + jnp.where(
                edge, jnp.where(at_south, column[0] + bottom, column[0]), 0.0
            )
            v[3][i] = v[3][i] + jnp.where(
                edge, jnp.where(at_north, top, pltpu.roll(column[0], rows - 1, 0)), 0.0
            )
        return v

    def keep_tiles(ref, where, tiles):
        for side in range(2):
            ref[(side,) + where] = tiles[side]

    small = [
        pltpu.make_async_copy(a, b, small_sem.at[n])
        for n, (a, b) in enumerate(
            (
                (jacobian_hbm, jacobian_ref),
                (metric_hbm, metric_ref),
                (turns_hbm, turns_ref),
                (viscosity_hbm, viscosity_ref),
            )
        )
    ]
    for c in small:
        c.start()

    def fields(g):
        part = (slice(None), slice(None), pl.ds(g * per, per))
        return [
            pltpu.make_async_copy(a.at[part], b.at[part], field_sem.at[n, g])
            for n, (a, b) in enumerate(
                ((state_hbm, state_ref), (forcing_hbm, forcing_ref))
            )
        ]

    for g in range(GROUPS):
        for c in fields(g):
            c.start()

    in_rows[...] = jnp.zeros_like(in_rows)
    in_tiles[...] = jnp.zeros_like(in_tiles)
    set_in_rows[...] = jnp.zeros_like(set_in_rows)
    set_in_tiles[...] = jnp.zeros_like(set_in_tiles)
    in_more[...] = jnp.zeros_like(in_more)
    ini_in_more[...] = jnp.zeros_like(ini_in_more)
    ini_in_rows[...] = jnp.zeros_like(ini_in_rows)
    ini_in_tiles[...] = jnp.zeros_like(ini_in_tiles)
    barrier = pltpu.get_barrier_semaphore()
    for_each(
        lambda d: pl.semaphore_signal(
            barrier, inc=1, device_id=device(d), device_id_type=MESH
        )
    )
    for c in small:
        c.wait()

    turns = turns_ref[...]
    masks = [turns == quarter for quarter in range(1, 4)]
    jacobian = face_frame(
        [[jacobian_ref[j, i] for i in range(NP)] for j in range(NP)], masks
    )
    metric = face_frame(
        [[metric_ref[j, i] for i in range(NP)] for j in range(NP)], masks
    )
    mass = [
        [float(weights[j] * weights[i]) * jacobian[j][i] for i in range(NP)]
        for j in range(NP)
    ]
    flux = [
        [float(weights[j] * weights[i]) * metric[j][i] for i in range(NP)]
        for j in range(NP)
    ]
    for j in range(NP):
        for i in range(NP):
            mass_ref[j * NP + i] = mass[j][i]

    def coefficients(f):
        return [
            sum(float(-derivative[n, a] * derivative[n, b]) * f[n] for n in range(NP))
            for a, b in PAIRS
        ]

    kx = [coefficients(flux[j]) for j in range(NP)]
    ky = [coefficients([flux[j][i] for j in range(NP)]) for i in range(NP)]
    for m in range(NP):
        for n in range(6):
            own_k_ref[m * 6 + n] = kx[m][n]
            own_k_ref[24 + m * 6 + n] = ky[m][n]
    first = lambda k: k[0] + k[1] + k[2]
    final = lambda k: k[2] + k[4] + k[5]
    dx = [[first(kx[j]), None, None, final(kx[j])] for j in range(NP)]
    dy = [[None] * NP for _ in range(NP)]
    for i in range(NP):
        dy[0][i], dy[3][i] = first(ky[i]), final(ky[i])
    dx, dy = joined_edges(dx, dy)
    local = join(mass)
    for n in range(NP):
        lay_rows(ini_out_rows, (0,), n, local[3][n], local[0][n])
        lay_rows(ini_out_rows, (0,), 4 + n, dy[3][n], dy[0][n])
    for n in range(6):
        lay_rows(ini_out_rows, (1,), n, kx[3][n], kx[0][n])
    for n in (6, 7):
        lay_rows(ini_out_rows, (1,), n, zero, zero)
    to_first, to_last = (0, 1, 2), (5, 4, 2)
    for side, i in ((0, 3), (1, 0)):
        to_corner = to_last if i == 3 else to_first
        columns = (
            [local[j][i] for j in range(NP)]
            + [dx[j][i] for j in range(NP)]
            + [ky[i][n] for n in range(6)]
            + [jnp.where(at_north, dx[3][i] + dy[3][i], dx[0][i] + dy[0][i])]
            + [
                stacked([kx[3][n] for n in to_corner], [kx[0][n] for n in to_corner]),
                along_x(local, i),
                stacked([ky[i][n] for n in to_last], [ky[i][n] for n in to_first]),
                along_y(local, i),
            ]
        )
        tile = zero
        for n, value in enumerate(columns):
            shift = (n + 1) % cols if i == 3 else n
            tile = jnp.where(lane == n, pltpu.roll(value, shift, 1), tile)
        ini_out_tiles[side] = tile
    for j in range(NP):
        for i in range(NP):
            inverse_ref[j * NP + i] = 1.0 / local[j][i]

    def enter_group(g):
        for c in fields(g):
            c.wait()

        def enter(c, carry):
            tiles, first = carry
            ch = g * per + c
            state = face_frame(load(state_ref, ch), masks)
            forcing = face_frame(load(forcing_ref, ch), masks)
            base = join(times(state, mass_ref))
            tend = join(times(forcing, mass_ref))
            store(base_ref, ch, base)
            store(tend_ref, ch, tend)
            tiles = emit(
                sets,
                (g,),
                c,
                tiles,
                ((base, base, corners_of(base)), (tend, tend, corners_of(tend))),
            )
            s = stiff(state, own_k_ref)
            store(part_ref, ch, s)
            rx, ry = from_inside(times(s, inverse_ref), own_k_ref)
            for j in (0, 3):
                at_row = at_north if j == 3 else at_south
                for i in (0, 3):
                    corner = at_row & (at_east if i == 3 else at_west)
                    rx[j][i] = jnp.where(corner, 0.0, rx[j][i])
                    ry[j][i] = jnp.where(corner, 0.0, ry[j][i])
            first = emit(
                main,
                (g,),
                c,
                first,
                ((s, s, None), (rx, ry, (zero,) * 4)),
                segments=True,
            )
            return tiles, first

        tiles, first = lax.fori_loop(
            0, per, enter, ((zero,) * 2, (zero,) * 2), unroll=UNROLL
        )
        keep_tiles(set_out_tiles, (g,), tiles)
        keep_tiles(out_tiles, (g,), first)

    def first_sends(g):
        start(main, (g,), (0, g), True)
        start(sets, (g,), (g,))

    @pl.loop(0, GROUPS)
    def _(g):
        enter_group(g)

        @pl.when(g == 1)
        def _():
            peers = (
                2 + 3 * there_north.astype(jnp.int32) + 3 * there_south.astype(jnp.int32)
            )
            pl.semaphore_wait(barrier, peers)
            start(ini, (), (), True)
            first_sends(0)

        @pl.when(g >= 1)
        def _():
            first_sends(g)

    finish(ini, (), (), True)
    got = [ini_in_tiles[d - 2] for d in range(2, 8)]
    beside = [[ini_in_more[v, side] for v in range(2)] for side in range(2)]
    CORNER_D, SEG = 14, 15

    def segment_weight(side, column):
        flank, above, below = [
            got[d - 2] for d in ((EAST, NE, SE) if side == 0 else (WEST, NW, SW))
        ]
        if column == SEG:
            total = flank + jnp.where(
                sub >= 5, pltpu.roll(above, 5, 0), pltpu.roll(below, 3, 0)
            )
        else:
            up, down = beside[side]
            total = jnp.where(
                sub >= 5, pltpu.roll(above + up, 5, 0), pltpu.roll(below + down, 3, 0)
            )
        k = jnp.broadcast_to(total[:, column : column + 1], (rows, cols))
        m = jnp.broadcast_to(total[:, column + 1 : column + 2], (rows, cols))
        used = (m > 0.0) & ((sub >= 5) | (sub <= 2))
        return jnp.where(used, k / jnp.where(used, m, 1.0), 0.0)

    for side in range(2):
        weight_ref[side, 0] = segment_weight(side, SEG)
        weight_ref[side, 1] = segment_weight(side, SEG + 2)

    def lane_of(d, n):
        to = last_col if d in (EAST, NE, SE) else 0
        return pltpu.roll(got[d - 2], (to - n) % cols, 1)

    def north(block, k):
        return jnp.where(at_north, row(ini_in_rows, (NORTH, block), k), 0.0)

    def south(block, k):
        return jnp.where(at_south, row(ini_in_rows, (SOUTH, block), k), 0.0)

    def east(n):
        return jnp.where(at_east, lane_of(EAST, n), 0.0)

    def west(n):
        return jnp.where(at_west, lane_of(WEST, n), 0.0)

    def with_neighbours(v, first_k, corner_up, corner_down):
        v = [list(r) for r in v]
        for i in range(NP):
            v[3][i] = v[3][i] + north(0, first_k + i)
            v[0][i] = v[0][i] + south(0, first_k + i)
        for j in range(NP):
            v[j][3] = v[j][3] + east(first_k + j)
            v[j][0] = v[j][0] + west(first_k + j)
        for d, j, i, m in (
            (NE, 3, 3, at_north & at_east),
            (SW, 0, 0, at_south & at_west),
            (NW, 3, 0, at_north & at_west),
            (SE, 0, 3, at_south & at_east),
        ):
            value = (
                pltpu.roll(lane_of(d, corner_up), rows - 1, 0)
                if j == 3
                else pltpu.roll(lane_of(d, corner_down), 1, 0)
            )
            v[j][i] = v[j][i] + jnp.where(m, value, 0.0)
        return v

    assembled = with_neighbours(local, 0, 0, 3)
    diagonal = with_neighbours([[zero] * NP for _ in range(NP)], 4, CORNER_D, CORNER_D)
    for j in range(NP):
        for i in range(NP):
            inverse_ref[j * NP + i] = 1.0 / assembled[j][i]
            diagonal_ref[j * NP + i] = diagonal[j][i]
    for m in range(NP):
        for n in range(6):
            x, y = kx[m][n], ky[m][n]
            if m == 0:
                x, y = x + south(1, n), y + west(8 + n)
            if m == 3:
                x, y = x + north(1, n), y + east(8 + n)
            both_k_ref[m * 6 + n] = x
            both_k_ref[24 + m * 6 + n] = y

    def emit_main(g, c, tiles, s):
        rx, ry = from_inside(times(s, inverse_ref), both_k_ref)
        corner = tuple(
            rx[j][i] + ry[j][i] for j, i in ((3, 3), (0, 0), (3, 0), (0, 3))
        )
        return emit(main, (g,), c, tiles, ((s, s, corners_of(s)), (rx, ry, corner)))

    def settle_group(g):
        finish(sets, (g,), (g,))
        got = in_sides(set_in_tiles, (g,))

        def settle(c, carry):
            ch = g * per + c
            for q, ref in enumerate((base_ref, tend_ref)):
                v = add_in(load(ref, ch), set_in_rows, (g,), c, got, q)
                store(ref, ch, times(v, inverse_ref))
            return carry

        lax.fori_loop(0, per, settle, 0, unroll=UNROLL)


    def advance(ch, c, g, parity, got, factor):
        where = (parity, g)
        s = add_in(load(part_ref, ch), in_rows, where, c, got, 0)
        w = times(s, inverse_ref)
        t = add_in(stiff(w, both_k_ref), in_rows, where, c, got, 1)
        scale = factor * viscosity_ref[ch]
        for j in range(NP):
            for i in range(NP):
                if j in (0, 3) or i in (0, 3):
                    t[j][i] = t[j][i] - diagonal_ref[j * NP + i] * w[j][i]
        return [
            [
                base_ref[j, i, ch]
                + (
                    factor * tend_ref[j, i, ch]
                    - scale * (t[j][i] * inverse_ref[j * NP + i])
                )
                for i in range(NP)
            ]
            for j in range(NP)
        ]

    def corner_shares(g):
        ends = (lane >= 6 * per) & (lane < 7 * per)
        for side, (flank, above, below) in enumerate(((EAST, NE, SE), (WEST, NW, SW))):
            here, up, down = [in_tiles[d - 2, 0, g] for d in (flank, above, below)]
            x = weight_ref[side, 0] * (
                here + jnp.where(sub >= 5, pltpu.roll(up, 5, 0), pltpu.roll(down, 3, 0))
            )
            y = weight_ref[side, 1] * jnp.where(
                sub >= 5,
                pltpu.roll(up + in_more[0, side, g], 5, 0),
                pltpu.roll(down + in_more[1, side, g], 3, 0),
            )
            share = pltpu.roll(x, cols - per, 1) + pltpu.roll(y, cols - 2 * per, 1)
            share = share + pltpu.roll(share, 1, 0) + pltpu.roll(share, 2, 0)
            in_tiles[flank - 2, 0, g] = jnp.where(
                ends & (sub == last_row - 1), pltpu.roll(share, rows - 1, 0), here
            )
            in_tiles[below - 2, 0, g] = jnp.where(
                ends & (sub == last_row - 2), pltpu.roll(share, 3, 0), down
            )

    def section_group(step):
        section, g = step // GROUPS, lax.rem(step, GROUPS)
        parity = lax.rem(section, 2)
        factor = jnp.float32(time_step / SECTIONS)
        for m in range(1, SECTIONS - 1):
            factor = jnp.where(
                section == m, jnp.float32(time_step / (SECTIONS - m)), factor
            )
        finish(main, (g,), (parity, g))

        @pl.when(section == 0)
        def _():
            finish_more(g)
            corner_shares(g)
            settle_group(g)

        got = in_sides(in_tiles, (parity, g))

        @pl.when(section == 0)
        def _():
            in_tiles[SE - 2, 0, g] = zero
            in_tiles[SW - 2, 0, g] = zero

        def body(c, tiles):
            ch = g * per + c
            u = advance(ch, c, g, parity, got, factor)
            s = stiff(u, own_k_ref)
            store(part_ref, ch, s)
            return emit_main(g, c, tiles, s)

        tiles = lax.fori_loop(0, per, body, (zero,) * 2, unroll=UNROLL)
        keep_tiles(out_tiles, (g,), tiles)
        start(main, (g,), (1 - parity, g))

    pl.loop(0, (SECTIONS - 1) * GROUPS)(section_group)

    def last_group(g):
        parity = (SECTIONS - 1) % 2
        finish(main, (g,), (parity, g))
        got = in_sides(in_tiles, (parity, g))

        def body(c, carry):
            ch = g * per + c
            store(out_ref, ch, advance(ch, c, g, parity, got, jnp.float32(time_step)))
            return carry

        lax.fori_loop(0, per, body, 0, unroll=UNROLL)

    pl.loop(0, GROUPS)(last_group)


def on_device(
    counts, initial_state, forcing, jacobian, metric, viscosity, element_turns
):
    np0, np1, chan, rows, cols = initial_state.shape
    per = chan // GROUPS
    f32 = jnp.float32
    field = pltpu.VMEM((NP, NP, chan, rows, cols), f32)
    vmem = pl.BlockSpec(memory_space=pltpu.VMEM)

    def buffers(out_lead, in_lead, tiles_per_rows, more):
        dma = pltpu.SemaphoreType.DMA
        tile = (rows, cols)
        got = [
            pltpu.VMEM((2,) + out_lead + (tiles_per_rows,) + tile, f32),
            pltpu.VMEM((2,) + out_lead + tile, f32),
            pltpu.VMEM((2,) + in_lead + (tiles_per_rows,) + tile, f32),
            pltpu.VMEM((6,) + in_lead + tile, f32),
        ]
        if more:
            got.append(pltpu.VMEM((2, 2) + out_lead + tile, f32))
        return got + [dma((10,) + out_lead), dma((10,) + in_lead)]

    return pl.pallas_call(
        functools.partial(kernel, (chan, rows, cols) + counts),
        out_shape=jax.ShapeDtypeStruct(initial_state.shape, f32),
        in_specs=[pl.BlockSpec(memory_space=pl.ANY)] * 6,
        out_specs=vmem,
        scratch_shapes=[
            field,
            field,
            pltpu.VMEM(jacobian.shape, f32),
            pltpu.VMEM(metric.shape, f32),
            pltpu.VMEM(element_turns.shape, jnp.int32),
            pltpu.SMEM(viscosity.shape, f32),
            pltpu.SemaphoreType.DMA((2, GROUPS)),
            pltpu.SemaphoreType.DMA((4,)),
            field,
            field,
            field,
            pltpu.VMEM((16, rows, cols), f32),
            pltpu.VMEM((48, rows, cols), f32),
            pltpu.VMEM((48, rows, cols), f32),
            pltpu.VMEM((16, rows, cols), f32),
            pltpu.VMEM((16, rows, cols), f32),
            pltpu.VMEM((2, 2, rows, cols), f32),
        ]
        + buffers((GROUPS,), (2, GROUPS), per, True)
        + buffers((GROUPS,), (GROUPS,), per, False)
        + buffers((), (), 2, True),
        compiler_params=pltpu.CompilerParams(
            collective_id=0, has_side_effects=True, vmem_limit_bytes=56 * 2**20
        ),
    )(initial_state, forcing, jacobian, metric, element_turns, viscosity)


def solution(mesh):
    placed = (
        P(None, None, None, "gy", "gx"),
        P(None, None, None, "gy", "gx"),
        P(None, None, "gy", "gx"),
        P(None, None, "gy", "gx"),
        P(),
        P("gy", "gx"),
    )
    return jax.shard_map(
        functools.partial(on_device, (mesh.shape["gx"], mesh.shape["gy"])),
        mesh=mesh,
        in_specs=placed,
        out_specs=P(None, None, None, "gy", "gx"),
        check_vma=False,
    )
```

```python
import functools
import math

import jax
import jax.numpy as jnp
import numpy as np
from jax import lax
from jax.experimental import pallas as pl
from jax.experimental.pallas import tpu as pltpu
from jax.sharding import PartitionSpec as P

NP = 4
SECTIONS = 5
GROUPS = 4
UNROLL = 8
time_step = 1.0
PAIRS = ((0, 1), (0, 2), (0, 3), (1, 2), (1, 3), (2, 3))
NORTH, SOUTH, EAST, WEST, NE, SW, NW, SE = range(8)
STEP = ((0, 1), (0, -1), (1, 0), (-1, 0), (1, 1), (-1, -1), (-1, 1), (1, -1))
MESH = pl.DeviceIdType.MESH
RIGHT = (EAST, NE, SE)
TILES_N, TILES_S = 8, 9


def lagrange_tables():
    root_five = 1.0 / math.sqrt(5.0)
    points = np.array([-1.0, -root_five, root_five, 1.0])
    weights = np.array([1.0 / 6.0, 5.0 / 6.0, 5.0 / 6.0, 1.0 / 6.0])
    number = points.shape[0]
    products = np.ones(number)
    for row in range(number):
        for other in range(number):
            if other != row:
                products[row] = products[row] * (points[row] - points[other])
    derivative = np.zeros((number, number))
    for row in range(number):
        for column in range(number):
            if row == column:
                derivative[row, column] = sum(
                    1.0 / (points[row] - points[other])
                    for other in range(number)
                    if other != row
                )
            else:
                derivative[row, column] = products[row] / (
                    products[column] * (points[row] - points[column])
                )
    return (derivative, weights)


def turned(v):
    return [[v[i][NP - 1 - j] for i in range(NP)] for j in range(NP)]


def face_frame(v, masks):
    result = v
    for mask in masks:
        v = turned(v)
        result = [
            [jnp.where(mask, v[j][i], result[j][i]) for i in range(NP)]
            for j in range(NP)
        ]
    return result


def kernel(
    sizes,
    state_hbm,
    forcing_hbm,
    jacobian_hbm,
    metric_hbm,
    turns_hbm,
    viscosity_hbm,
    out_ref,
    state_ref,
    forcing_ref,
    jacobian_ref,
    metric_ref,
    turns_ref,
    viscosity_ref,
    field_sem,
    small_sem,
    part_ref,
    base_ref,
    tend_ref,
    inverse_ref,
    own_k_ref,
    both_k_ref,
    diagonal_ref,
    mass_ref,
    weight_ref,
    inner_ref,
    out_rows,
    out_tiles,
    in_rows,
    in_tiles,
    in_more,
    send_sem,
    recv_sem,
    set_out_rows,
    set_out_tiles,
    set_in_rows,
    set_in_tiles,
    set_send,
    set_recv,
    ini_out_rows,
    ini_out_tiles,
    ini_in_rows,
    ini_in_tiles,
    ini_in_more,
    ini_send,
    ini_recv,
):
    chan, rows, cols, count_x, count_y = sizes
    per = chan // GROUPS
    last_row, last_col = rows - 1, cols - 1
    derivative, weights = lagrange_tables()
    cx = lax.axis_index("gx")
    cy = lax.axis_index("gy")
    lane = lax.broadcasted_iota(jnp.int32, (rows, cols), 1)
    sub = lax.broadcasted_iota(jnp.int32, (rows, cols), 0)
    at_west, at_east = lane == 0, lane == last_col
    at_south, at_north = sub == 0, sub == last_row
    zero = jnp.zeros((rows, cols), jnp.float32)
    there_north = cy < count_y - 1
    there_south = cy > 0

    def device(d):
        dx, dy = STEP[d % 8]
        return (lax.rem(cx + dx + count_x, count_x), cy + dy)

    def for_each(todo, tiles_too=False):
        @pl.when(there_north)
        def _():
            for d in (NE, NW, NORTH) + (TILES_N,) * tiles_too:
                todo(d)

        @pl.when(there_south)
        def _():
            for d in (SE, SW, SOUTH) + (TILES_S,) * tiles_too:
                todo(d)

        for d in (EAST, WEST):
            todo(d)

    def copy(bufs, where_out, where_in, d, arriving=False):
        o_rows, o_tiles, i_rows, i_tiles, i_more, ssem, rsem = bufs
        slot = d if arriving else d ^ 1
        send, recv = ssem.at[(d,) + where_out], rsem.at[(slot,) + where_in]
        if d in (NORTH, SOUTH):
            src, dst = o_rows.at[(d,) + where_out], i_rows.at[(slot,) + where_in]
        elif d in (TILES_N, TILES_S):
            src = o_tiles.at[(slice(None),) + where_out]
            dst = i_more.at[(slot - 8, slice(None)) + where_out]
            recv = rsem.at[(slot,) + where_in]
        else:
            src = o_tiles.at[(int(d not in RIGHT),) + where_out]
            dst = i_tiles.at[(slot - 2,) + where_in]
        return pltpu.make_async_remote_copy(
            src_ref=src,
            dst_ref=dst,
            send_sem=send,
            recv_sem=recv,
            device_id=device(d),
            device_id_type=MESH,
        )

    def start(bufs, where_out, where_in, tiles_too=False):
        for_each(lambda d: copy(bufs, where_out, where_in, d).start(), tiles_too)

    def finish(bufs, where_out, where_in, tiles_too=False):
        def todo(d):
            c = copy(bufs, where_out, where_in, d, arriving=True)
            c.wait_recv()
            c.wait_send()

        for_each(todo, tiles_too)

    def finish_more(g):
        def todo(d):
            if d in (TILES_N, TILES_S):
                c = copy(main, (g,), (0, g), d, arriving=True)
                c.wait_recv()
                c.wait_send()

        for_each(todo, True)

    main = (out_rows, out_tiles, in_rows, in_tiles, in_more, send_sem, recv_sem)
    sets = (
        set_out_rows, set_out_tiles, set_in_rows, set_in_tiles, None, set_send, set_recv
    )
    ini = (
        ini_out_rows, ini_out_tiles, ini_in_rows, ini_in_tiles, ini_in_more,
        ini_send, ini_recv,
    )

    def join_x(a, b):
        return (
            a + jnp.where(at_west, 0.0, pltpu.roll(b, 1, 1)),
            b + jnp.where(at_east, 0.0, pltpu.roll(a, cols - 1, 1)),
        )

    def join_y(a, b):
        return (
            a + jnp.where(at_south, 0.0, pltpu.roll(b, 1, 0)),
            b + jnp.where(at_north, 0.0, pltpu.roll(a, rows - 1, 0)),
        )

    def join(s):
        s = [list(r) for r in s]
        for j in range(NP):
            s[j][0], s[j][3] = join_x(s[j][0], s[j][3])
        for i in range(NP):
            s[0][i], s[3][i] = join_y(s[0][i], s[3][i])
        return s

    def line(v, k):
        p = [k[n] * (v[b] - v[a]) for n, (a, b) in enumerate(PAIRS)]
        return (
            p[0] + p[1] + p[2],
            p[3] + p[4] - p[0],
            p[5] - p[1] - p[3],
            -(p[2] + p[4] + p[5]),
        )

    def stiff(v, k_ref):
        s = [[None] * NP for _ in range(NP)]
        for j in range(NP):
            got = line(v[j], [k_ref[j * 6 + n] for n in range(6)])
            for i in range(NP):
                s[j][i] = got[i]
        for i in range(NP):
            got = line(
                [v[j][i] for j in range(NP)],
                [k_ref[24 + i * 6 + n] for n in range(6)],
            )
            for j in range(NP):
                s[j][i] = s[j][i] + got[j]
        return join(s)

    def inner_coefficients(kx, ky):
        fields = []
        for lines, far in ((kx, at_east), (ky, at_north)):
            for k in lines:
                to_first = (zero, k[0], k[1], k[2])
                to_last = (k[2], k[4], k[5], zero)
                fields += [jnp.where(far, b, a) for a, b in zip(to_first, to_last)]
        return fields

    def from_inside(w):
        def total(m, v):
            k = [inner_ref[m * NP + n] for n in range(NP)]
            return k[0] * v[0] + k[1] * v[1] + k[2] * v[2] + k[3] * v[3]

        x = [total(j, w[j]) for j in range(NP)]
        y = [total(NP + i, [w[j][i] for j in range(NP)]) for i in range(NP)]
        x[0], x[3] = join_y(x[0], x[3])
        y[0], y[3] = join_x(y[0], y[3])
        return [[v] * NP for v in x], [list(y) for _ in range(NP)]

    def joined_edges(rx, ry):
        for i in (0, 3):
            rx[0][i], rx[3][i] = join_y(rx[0][i], rx[3][i])
        for j in (0, 3):
            ry[j][0], ry[j][3] = join_x(ry[j][0], ry[j][3])
        return rx, ry

    def load(ref, c):
        return [[ref[j, i, c] for i in range(NP)] for j in range(NP)]

    def store(ref, c, v):
        for j in range(NP):
            for i in range(NP):
                ref[j, i, c] = v[j][i]

    def times(v, ref):
        return [[v[j][i] * ref[j * NP + i] for i in range(NP)] for j in range(NP)]

    def lay_rows(ref, where, k, top, bottom):
        ref[(NORTH,) + where + (slice(k, k + 1), slice(None))] = top[last_row:, :]
        ref[(SOUTH,) + where + (slice(k, k + 1), slice(None))] = bottom[0:1, :]

    def lay_lane(tiles, n, right, left, corner):
        here = lane == n
        from_right = lax.rem(n + 1, cols)

        def put(d, v, shift):
            tiles[d - 2] = jnp.where(here, pltpu.roll(v, shift, 1), tiles[d - 2])

        if right is not None:
            put(EAST, right, from_right)
            put(WEST, left, n)
        if corner is not None:
            put(NE, corner[0], from_right)
            put(SW, corner[1], n)
            put(NW, corner[2], n)
            put(SE, corner[3], from_right)

    def stacked(top, bottom):
        kept = top[0]
        for n in (1, 2):
            kept = jnp.where(sub == last_row - n, pltpu.roll(top[n], rows - n, 0), kept)
        for n in range(3):
            kept = jnp.where(sub == 2 - n, pltpu.roll(bottom[n], 2 - n, 0), kept)
        return kept

    def along_x(v, i):
        order = (2, 1, 0) if i == 3 else (1, 2, 3)
        return stacked([v[3][n] for n in order], [v[0][n] for n in order])

    def along_y(v, i):
        return stacked([v[n][i] for n in (2, 1, 0)], [v[n][i] for n in (1, 2, 3)])

    def emit(refs, where, c, tiles, fields, segments=False):
        for q, (vx, vy, corner) in enumerate(fields):
            for i in range(NP):
                lay_rows(refs[0], where + (c,), q * NP + i, vy[3][i], vy[0][i])
        sides = []
        for tile, i in zip(tiles, (3, 0)):
            (v, _, _), (x, _, corner) = fields
            top, bottom = (corner[0], corner[3]) if i == 3 else (corner[2], corner[1])
            ends = jnp.where(
                sub == last_row,
                v[3][i],
                jnp.where(
                    sub == last_row - 1,
                    pltpu.roll(x[3][i], rows - 1, 0),
                    jnp.where(sub == last_row - 2, pltpu.roll(top, rows - 2, 0), bottom),
                ),
            )
            columns = [f[0][j][i] for f in fields for j in range(3)] + [ends]
            if segments:
                columns += [along_x(v, i), along_y(v, i)]
            for m, value in enumerate(columns):
                n = m * per + c
                shift = lax.rem(n + 1, cols) if i == 3 else n
                tile = jnp.where(lane == n, pltpu.roll(value, shift, 1), tile)
            sides.append(tile)
        return tuple(sides)

    def corners_of(v):
        return (v[3][3], v[0][0], v[3][0], v[0][3])

    def row(ref, where, k):
        return jnp.broadcast_to(
            ref[where + (slice(k, k + 1), slice(None))], (rows, cols)
        )

    def in_sides(ref, where):
        sides = []
        for side, above, below in ((EAST, NE, SE), (WEST, NW, SW)):
            here, up, down = [ref[(d - 2,) + where] for d in (side, above, below)]
            first = pltpu.roll(pltpu.roll(up, 6 * per, 1), rows - 1, 0)
            ends = jnp.where(
                sub == last_row,
                here + first,
                jnp.where(
                    sub == last_row - 1,
                    here + pltpu.roll(up, rows - 2, 0),
                    jnp.where(sub == 0, pltpu.roll(down, 1, 0), pltpu.roll(down, 4, 0)),
                ),
            )
            sides.append(jnp.where(lane < 6 * per, here, ends))
        return sides

    def add_in(v, ref, where, c, got, q):
        v = [list(r) for r in v]
        for i in range(NP):
            k = q * NP + i
            v[3][i] = v[3][i] + jnp.where(at_north, row(ref, (NORTH,) + where + (c,), k), 0.0)
            v[0][i] = v[0][i] + jnp.where(at_south, row(ref, (SOUTH,) + where + (c,), k), 0.0)
        for side, i, to, edge in ((0, 3, last_col, at_east), (1, 0, cols, at_west)):

            def lane_to(m):
                return pltpu.roll(got[side], lax.rem(to - (m * per + c), cols), 1)

            column = [lane_to(q * 3 + j) for j in range(3)]
            ends = lane_to(6)
            if q == 1:
                top, bottom = pltpu.roll(ends, 1, 0), pltpu.roll(ends, rows - 1, 0)
            else:
                top = bottom = ends
            for j in (1, 2):
                v[j][i] = v[j][i] + jnp.where(edge, column[j], 0.0)
            v[0][i] = v[0][i] + jnp.where(
                edge, jnp.where(at_south, column[0] + bottom, column[0]), 0.0
            )
            v[3][i] = v[3][i] + jnp.where(
                edge, jnp.where(at_north, top, pltpu.roll(column[0], rows - 1, 0)), 0.0
            )
        return v

    def keep_tiles(ref, where, tiles):
        for side in range(2):
            ref[(side,) + where] = tiles[side]

    small = [
        pltpu.make_async_copy(a, b, small_sem.at[n])
        for n, (a, b) in enumerate(
            (
                (jacobian_hbm, jacobian_ref),
                (metric_hbm, metric_ref),
                (turns_hbm, turns_ref),
                (viscosity_hbm, viscosity_ref),
            )
        )
    ]
    for c in small:
        c.start()

    def fields(g):
        part = (slice(None), slice(None), pl.ds(g * per, per))
        return [
            pltpu.make_async_copy(a.at[part], b.at[part], field_sem.at[n, g])
            for n, (a, b) in enumerate(
                ((state_hbm, state_ref), (forcing_hbm, forcing_ref))
            )
        ]

    for g in range(GROUPS):
        for c in fields(g):
            c.start()

    in_rows[...] = jnp.zeros_like(in_rows)
    in_tiles[...] = jnp.zeros_like(in_tiles)
    set_in_rows[...] = jnp.zeros_like(set_in_rows)
    set_in_tiles[...] = jnp.zeros_like(set_in_tiles)
    in_more[...] = jnp.zeros_like(in_more)
    ini_in_more[...] = jnp.zeros_like(ini_in_more)
    ini_in_rows[...] = jnp.zeros_like(ini_in_rows)
    ini_in_tiles[...] = jnp.zeros_like(ini_in_tiles)
    barrier = pltpu.get_barrier_semaphore()
    for_each(
        lambda d: pl.semaphore_signal(
            barrier, inc=1, device_id=device(d), device_id_type=MESH
        )
    )
    for c in small:
        c.wait()

    turns = turns_ref[...]
    masks = [turns == quarter for quarter in range(1, 4)]
    jacobian = face_frame(
        [[jacobian_ref[j, i] for i in range(NP)] for j in range(NP)], masks
    )
    metric = face_frame(
        [[metric_ref[j, i] for i in range(NP)] for j in range(NP)], masks
    )
    mass = [
        [float(weights[j] * weights[i]) * jacobian[j][i] for i in range(NP)]
        for j in range(NP)
    ]
    flux = [
        [float(weights[j] * weights[i]) * metric[j][i] for i in range(NP)]
        for j in range(NP)
    ]
    for j in range(NP):
        for i in range(NP):
            mass_ref[j * NP + i] = mass[j][i]

    def coefficients(f):
        return [
            sum(float(-derivative[n, a] * derivative[n, b]) * f[n] for n in range(NP))
            for a, b in PAIRS
        ]

    kx = [coefficients(flux[j]) for j in range(NP)]
    ky = [coefficients([flux[j][i] for j in range(NP)]) for i in range(NP)]
    for m in range(NP):
        for n in range(6):
            own_k_ref[m * 6 + n] = kx[m][n]
            own_k_ref[24 + m * 6 + n] = ky[m][n]
    first = lambda k: k[0] + k[1] + k[2]
    final = lambda k: k[2] + k[4] + k[5]
    dx = [[first(kx[j]), None, None, final(kx[j])] for j in range(NP)]
    dy = [[None] * NP for _ in range(NP)]
    for i in range(NP):
        dy[0][i], dy[3][i] = first(ky[i]), final(ky[i])
    dx, dy = joined_edges(dx, dy)
    local = join(mass)
    for n in range(NP):
        lay_rows(ini_out_rows, (0,), n, local[3][n], local[0][n])
        lay_rows(ini_out_rows, (0,), 4 + n, dy[3][n], dy[0][n])
    for n in range(6):
        lay_rows(ini_out_rows, (1,), n, kx[3][n], kx[0][n])
    for n in (6, 7):
        lay_rows(ini_out_rows, (1,), n, zero, zero)
    to_first, to_last = (0, 1, 2), (5, 4, 2)
    for side, i in ((0, 3), (1, 0)):
        to_corner = to_last if i == 3 else to_first
        columns = (
            [local[j][i] for j in range(NP)]
            + [dx[j][i] for j in range(NP)]
            + [ky[i][n] for n in range(6)]
            + [jnp.where(at_north, dx[3][i] + dy[3][i], dx[0][i] + dy[0][i])]
            + [
                stacked([kx[3][n] for n in to_corner], [kx[0][n] for n in to_corner]),
                along_x(local, i),
                stacked([ky[i][n] for n in to_last], [ky[i][n] for n in to_first]),
                along_y(local, i),
            ]
        )
        tile = zero
        for n, value in enumerate(columns):
            shift = (n + 1) % cols if i == 3 else n
            tile = jnp.where(lane == n, pltpu.roll(value, shift, 1), tile)
        ini_out_tiles[side] = tile
    for j in range(NP):
        for i in range(NP):
            inverse_ref[j * NP + i] = 1.0 / local[j][i]
    for n, value in enumerate(inner_coefficients(kx, ky)):
        inner_ref[n] = value

    def enter_group(g):
        for c in fields(g):
            c.wait()

        def enter(c, carry):
            tiles, first = carry
            ch = g * per + c
            state = face_frame(load(state_ref, ch), masks)
            forcing = face_frame(load(forcing_ref, ch), masks)
            base = join(times(state, mass_ref))
            tend = join(times(forcing, mass_ref))
            store(base_ref, ch, base)
            store(tend_ref, ch, tend)
            tiles = emit(
                sets,
                (g,),
                c,
                tiles,
                ((base, base, corners_of(base)), (tend, tend, corners_of(tend))),
            )
            s = stiff(state, own_k_ref)
            store(part_ref, ch, s)
            rx, ry = from_inside(times(s, inverse_ref))
            for j in (0, 3):
                at_row = at_north if j == 3 else at_south
                for i in (0, 3):
                    corner = at_row & (at_east if i == 3 else at_west)
                    rx[j][i] = jnp.where(corner, 0.0, rx[j][i])
                    ry[j][i] = jnp.where(corner, 0.0, ry[j][i])
            first = emit(
                main,
                (g,),
                c,
                first,
                ((s, s, None), (rx, ry, (zero,) * 4)),
                segments=True,
            )
            return tiles, first

        tiles, first = lax.fori_loop(
            0, per, enter, ((zero,) * 2, (zero,) * 2), unroll=UNROLL
        )
        keep_tiles(set_out_tiles, (g,), tiles)
        keep_tiles(out_tiles, (g,), first)

    def first_sends(g):
        start(main, (g,), (0, g), True)
        start(sets, (g,), (g,))

    @pl.loop(0, GROUPS)
    def _(g):
        enter_group(g)

        @pl.when(g == 1)
        def _():
            peers = (
                2 + 3 * there_north.astype(jnp.int32) + 3 * there_south.astype(jnp.int32)
            )
            pl.semaphore_wait(barrier, peers)
            start(ini, (), (), True)
            first_sends(0)

        @pl.when(g >= 1)
        def _():
            first_sends(g)

    finish(ini, (), (), True)
    got = [ini_in_tiles[d - 2] for d in range(2, 8)]
    beside = [[ini_in_more[v, side] for v in range(2)] for side in range(2)]
    CORNER_D, SEG = 14, 15

    def segment_weight(side, column):
        flank, above, below = [
            got[d - 2] for d in ((EAST, NE, SE) if side == 0 else (WEST, NW, SW))
        ]
        if column == SEG:
            total = flank + jnp.where(
                sub >= 5, pltpu.roll(above, 5, 0), pltpu.roll(below, 3, 0)
            )
        else:
            up, down = beside[side]
            total = jnp.where(
                sub >= 5, pltpu.roll(above + up, 5, 0), pltpu.roll(below + down, 3, 0)
            )
        k = jnp.broadcast_to(total[:, column : column + 1], (rows, cols))
        m = jnp.broadcast_to(total[:, column + 1 : column + 2], (rows, cols))
        used = (m > 0.0) & ((sub >= 5) | (sub <= 2))
        return jnp.where(used, k / jnp.where(used, m, 1.0), 0.0)

    for side in range(2):
        weight_ref[side, 0] = segment_weight(side, SEG)
        weight_ref[side, 1] = segment_weight(side, SEG + 2)

    def lane_of(d, n):
        to = last_col if d in (EAST, NE, SE) else 0
        return pltpu.roll(got[d - 2], (to - n) % cols, 1)

    def north(block, k):
        return jnp.where(at_north, row(ini_in_rows, (NORTH, block), k), 0.0)

    def south(block, k):
        return jnp.where(at_south, row(ini_in_rows, (SOUTH, block), k), 0.0)

    def east(n):
        return jnp.where(at_east, lane_of(EAST, n), 0.0)

    def west(n):
        return jnp.where(at_west, lane_of(WEST, n), 0.0)

    def with_neighbours(v, first_k, corner_up, corner_down):
        v = [list(r) for r in v]
        for i in range(NP):
            v[3][i] = v[3][i] + north(0, first_k + i)
            v[0][i] = v[0][i] + south(0, first_k + i)
        for j in range(NP):
            v[j][3] = v[j][3] + east(first_k + j)
            v[j][0] = v[j][0] + west(first_k + j)
        for d, j, i, m in (
            (NE, 3, 3, at_north & at_east),
            (SW, 0, 0, at_south & at_west),
            (NW, 3, 0, at_north & at_west),
            (SE, 0, 3, at_south & at_east),
        ):
            value = (
                pltpu.roll(lane_of(d, corner_up), rows - 1, 0)
                if j == 3
                else pltpu.roll(lane_of(d, corner_down), 1, 0)
            )
            v[j][i] = v[j][i] + jnp.where(m, value, 0.0)
        return v

    assembled = with_neighbours(local, 0, 0, 3)
    diagonal = with_neighbours([[zero] * NP for _ in range(NP)], 4, CORNER_D, CORNER_D)
    for j in range(NP):
        for i in range(NP):
            inverse_ref[j * NP + i] = 1.0 / assembled[j][i]
            diagonal_ref[j * NP + i] = diagonal[j][i]
    both_x, both_y = [list(k) for k in kx], [list(k) for k in ky]
    for n in range(6):
        both_x[0][n] = both_x[0][n] + south(1, n)
        both_x[3][n] = both_x[3][n] + north(1, n)
        both_y[0][n] = both_y[0][n] + west(8 + n)
        both_y[3][n] = both_y[3][n] + east(8 + n)
    for m in range(NP):
        for n in range(6):
            both_k_ref[m * 6 + n] = both_x[m][n]
            both_k_ref[24 + m * 6 + n] = both_y[m][n]
    for n, value in enumerate(inner_coefficients(both_x, both_y)):
        inner_ref[n] = value

    def emit_main(g, c, tiles, s):
        rx, ry = from_inside(times(s, inverse_ref))
        corner = tuple(
            rx[j][i] + ry[j][i] for j, i in ((3, 3), (0, 0), (3, 0), (0, 3))
        )
        return emit(main, (g,), c, tiles, ((s, s, corners_of(s)), (rx, ry, corner)))

    def settle_group(g):
        finish(sets, (g,), (g,))
        got = in_sides(set_in_tiles, (g,))

        def settle(c, carry):
            ch = g * per + c
            for q, ref in enumerate((base_ref, tend_ref)):
                v = add_in(load(ref, ch), set_in_rows, (g,), c, got, q)
                store(ref, ch, times(v, inverse_ref))
            return carry

        lax.fori_loop(0, per, settle, 0, unroll=UNROLL)


    def advance(ch, c, g, parity, got, factor):
        where = (parity, g)
        s = add_in(load(part_ref, ch), in_rows, where, c, got, 0)
        w = times(s, inverse_ref)
        t = add_in(stiff(w, both_k_ref), in_rows, where, c, got, 1)
        scale = factor * viscosity_ref[ch]
        for j in range(NP):
            for i in range(NP):
                if j in (0, 3) or i in (0, 3):
                    t[j][i] = t[j][i] - diagonal_ref[j * NP + i] * w[j][i]
        return [
            [
                base_ref[j, i, ch]
                + (
                    factor * tend_ref[j, i, ch]
                    - scale * (t[j][i] * inverse_ref[j * NP + i])
                )
                for i in range(NP)
            ]
            for j in range(NP)
        ]

    def corner_shares(g):
        ends = (lane >= 6 * per) & (lane < 7 * per)
        for side, (flank, above, below) in enumerate(((EAST, NE, SE), (WEST, NW, SW))):
            here, up, down = [in_tiles[d - 2, 0, g] for d in (flank, above, below)]
            x = weight_ref[side, 0] * (
                here + jnp.where(sub >= 5, pltpu.roll(up, 5, 0), pltpu.roll(down, 3, 0))
            )
            y = weight_ref[side, 1] * jnp.where(
                sub >= 5,
                pltpu.roll(up + in_more[0, side, g], 5, 0),
                pltpu.roll(down + in_more[1, side, g], 3, 0),
            )
            share = pltpu.roll(x, cols - per, 1) + pltpu.roll(y, cols - 2 * per, 1)
            share = share + pltpu.roll(share, 1, 0) + pltpu.roll(share, 2, 0)
            in_tiles[flank - 2, 0, g] = jnp.where(
                ends & (sub == last_row - 1), pltpu.roll(share, rows - 1, 0), here
            )
            in_tiles[below - 2, 0, g] = jnp.where(
                ends & (sub == last_row - 2), pltpu.roll(share, 3, 0), down
            )

    def section_group(step):
        section, g = step // GROUPS, lax.rem(step, GROUPS)
        parity = lax.rem(section, 2)
        factor = jnp.float32(time_step / SECTIONS)
        for m in range(1, SECTIONS - 1):
            factor = jnp.where(
                section == m, jnp.float32(time_step / (SECTIONS - m)), factor
            )
        finish(main, (g,), (parity, g))

        @pl.when(section == 0)
        def _():
            finish_more(g)
            corner_shares(g)
            settle_group(g)

        got = in_sides(in_tiles, (parity, g))

        @pl.when(section == 0)
        def _():
            in_tiles[SE - 2, 0, g] = zero
            in_tiles[SW - 2, 0, g] = zero

        def body(c, tiles):
            ch = g * per + c
            u = advance(ch, c, g, parity, got, factor)
            s = stiff(u, own_k_ref)
            store(part_ref, ch, s)
            return emit_main(g, c, tiles, s)

        tiles = lax.fori_loop(0, per, body, (zero,) * 2, unroll=UNROLL)
        keep_tiles(out_tiles, (g,), tiles)
        start(main, (g,), (1 - parity, g))

    pl.loop(0, (SECTIONS - 1) * GROUPS)(section_group)

    def last_group(g):
        parity = (SECTIONS - 1) % 2
        finish(main, (g,), (parity, g))
        got = in_sides(in_tiles, (parity, g))

        def body(c, carry):
            ch = g * per + c
            store(out_ref, ch, advance(ch, c, g, parity, got, jnp.float32(time_step)))
            return carry

        lax.fori_loop(0, per, body, 0, unroll=UNROLL)

    pl.loop(0, GROUPS)(last_group)


def on_device(
    counts, initial_state, forcing, jacobian, metric, viscosity, element_turns
):
    np0, np1, chan, rows, cols = initial_state.shape
    per = chan // GROUPS
    f32 = jnp.float32
    field = pltpu.VMEM((NP, NP, chan, rows, cols), f32)
    vmem = pl.BlockSpec(memory_space=pltpu.VMEM)

    def buffers(out_lead, in_lead, tiles_per_rows, more):
        dma = pltpu.SemaphoreType.DMA
        tile = (rows, cols)
        got = [
            pltpu.VMEM((2,) + out_lead + (tiles_per_rows,) + tile, f32),
            pltpu.VMEM((2,) + out_lead + tile, f32),
            pltpu.VMEM((2,) + in_lead + (tiles_per_rows,) + tile, f32),
            pltpu.VMEM((6,) + in_lead + tile, f32),
        ]
        if more:
            got.append(pltpu.VMEM((2, 2) + out_lead + tile, f32))
        return got + [dma((10,) + out_lead), dma((10,) + in_lead)]

    return pl.pallas_call(
        functools.partial(kernel, (chan, rows, cols) + counts),
        out_shape=jax.ShapeDtypeStruct(initial_state.shape, f32),
        in_specs=[pl.BlockSpec(memory_space=pl.ANY)] * 6,
        out_specs=vmem,
        scratch_shapes=[
            field,
            field,
            pltpu.VMEM(jacobian.shape, f32),
            pltpu.VMEM(metric.shape, f32),
            pltpu.VMEM(element_turns.shape, jnp.int32),
            pltpu.SMEM(viscosity.shape, f32),
            pltpu.SemaphoreType.DMA((2, GROUPS)),
            pltpu.SemaphoreType.DMA((4,)),
            field,
            field,
            field,
            pltpu.VMEM((16, rows, cols), f32),
            pltpu.VMEM((48, rows, cols), f32),
            pltpu.VMEM((48, rows, cols), f32),
            pltpu.VMEM((16, rows, cols), f32),
            pltpu.VMEM((16, rows, cols), f32),
            pltpu.VMEM((2, 2, rows, cols), f32),
            pltpu.VMEM((32, rows, cols), f32),
        ]
        + buffers((GROUPS,), (2, GROUPS), per, True)
        + buffers((GROUPS,), (GROUPS,), per, False)
        + buffers((), (), 2, True),
        compiler_params=pltpu.CompilerParams(
            collective_id=0, has_side_effects=True, vmem_limit_bytes=56 * 2**20
        ),
    )(initial_state, forcing, jacobian, metric, element_turns, viscosity)


def solution(mesh):
    placed = (
        P(None, None, None, "gy", "gx"),
        P(None, None, None, "gy", "gx"),
        P(None, None, "gy", "gx"),
        P(None, None, "gy", "gx"),
        P(),
        P("gy", "gx"),
    )
    return jax.shard_map(
        functools.partial(on_device, (mesh.shape["gx"], mesh.shape["gy"])),
        mesh=mesh,
        in_specs=placed,
        out_specs=P(None, None, None, "gy", "gx"),
        check_vma=False,
    )
```
